256 devices in a mesh: ctx: 32 (over y, x, core), tp: 4 (over z_hi), dp: 2 (over z_lo).
Axes of the slice: x: 4, y: 4, z: 8 (z_hi: 4, z_lo: 2; z = z_hi * 2 + z_lo), core: 2. Of those that a mesh axis runs over, the one named last changes fastest.
Arguments:
- head_input: float32 [2, 7168, 2560], P('dp', 'ctx', 'tp'), may hold values from -24 to 24
- gate_input: float32 [2, 7168, 2560], P('dp', 'ctx', 'tp'), may hold values from -5 to 5
- log_decay: float32 [2, 40, 7168], P('dp', 'tp', 'ctx'), may hold values from -0.8 to 0, as said below
- in_b: float32 [2, 7168, 128], P('dp', 'ctx'), may hold values from -0.5 to 0.5
- in_c: float32 [2, 7168, 128], P('dp', 'ctx'), may hold values from -0.1875 to 0.1875
- skip: float32 [40], P('tp'), may hold values from 0.5 to 2
- norm_gain: float32 [2560], P('tp'), may hold values from 0.25 to 1.75
- w_out: float32 [2560, 2560], P('tp'), may hold values from -0.125 to 0.125
- d_out: float32 [2, 7168, 2560], P('dp', ('ctx', 'tp')), may hold values from -24 to 24
Outputs:
- out: float32 [2, 7168, 2560], P('dp', ('ctx', 'tp'))
- grad_input: float32 [2, 7168, 2560], P('dp', 'ctx', 'tp')
- grad_w_out_t: float32 [2560, 2560], P(('ctx', 'dp'), 'tp')
The draws below stay inside these ranges and needn't reach their ends.
Inputs may be any that keep to these rules, and one draw needn't show every extreme that they name: `log_decay`: every entry is negative.
All inputs are finite; a program needn't handle non-finite values.
Results may differ from the reference program's by a relative error of at most 0.00023.
Values sent between devices are 32-bit elements; how exact they have to be, the bound alone decides.
No kernel may reach another device: no remote copies, remote signals or barrier semaphores. Data moves between devices by JAX's collectives and lax.ppermute only.
A program may use at most 128 MiB of HBM per device.

```python
import math
import jax
import jax.numpy as jnp
from jax import lax

D = 2560
HEADS = 40
HEAD = 64
STATE = 128
GROUP = 640
TOK_DEV = 224
SEQS = 2
SEQLEN = 7168
INNER = 2560


def draw_head_input(key, part):
    keys = jax.random.split(key, 3)
    shape = (SEQS, SEQLEN, HEADS * HEAD)
    channel_scale = jnp.exp(jax.random.uniform(keys[0], (1, 1, HEADS * HEAD), jnp.float32, math.log(0.3), math.log(3.0)))
    token_scale = jnp.exp(jax.random.uniform(keys[1], (SEQS, SEQLEN, 1), jnp.float32, math.log(0.5), math.log(2.0)))
    base = jnp.clip(jax.random.normal(keys[2], shape, jnp.float32), -4.0, 4.0)
    return (base * channel_scale * token_scale).astype(jnp.float32)


def draw_log_decay(key, part):
    keys = jax.random.split(key, 6)
    shape = (SEQS, HEADS, SEQLEN)
    quick = jax.random.randint(keys[0], (SEQS, HEADS, 1), 0, 2) == 0
    slow_rate = jax.random.uniform(keys[1], (SEQS, HEADS, 1), jnp.float32, 0.1, 0.8) / SEQLEN
    fast_rate = 1.0 / jax.random.uniform(keys[2], (SEQS, HEADS, 1), jnp.float32, 30.0, 50.0)
    rough = jnp.exp(jax.random.uniform(keys[3], shape, jnp.float32, math.log(0.5), math.log(2.0)))
    decay_rate = jnp.where(quick, fast_rate, slow_rate) * rough
    sample_positions = jax.random.randint(keys[4], (SEQS, 1, 1, 2), 0, SEQLEN)
    location_list = jnp.arange(SEQLEN, dtype=jnp.int32)[None, None, :, None]
    spike_amplitude = jnp.any(location_list == sample_positions, axis=3)
    loss_values = jnp.log(jax.random.uniform(keys[5], shape, jnp.float32, 0.5, 0.8))
    return (jnp.where(spike_amplitude, loss_values, 0.0) - decay_rate).astype(jnp.float32)


def spiked(drawn, key, source, target, blocks, factor):
    owner, partner = [(jnp.arange(drawn.shape[position]) // (drawn.shape[position] // blocks)).reshape([-1 if axis == position else 1 for axis in range(drawn.ndim)]) for position in (source, target)]
    chosen = jax.random.permutation(key, blocks)[partner]
    strong = (owner == chosen) | (owner == (partner + blocks // 2) % blocks)
    return jnp.where(strong, factor * drawn, drawn)


def level_of(stream_key, extent, shards, low, high):
    level, own = 1.0, jax.random.fold_in(stream_key, 6)
    for position, blocks in shards:
        steps = jnp.exp(jax.random.uniform(jax.random.fold_in(own, position), (blocks,), jnp.float32, low / len(shards), high / len(shards)))
        level = level * jnp.repeat(steps, extent[position] // blocks).reshape([-1 if axis == position else 1 for axis in range(len(extent))])
    return level


def bell_draw(key, shape, width, reach, cuts=(), held_as=jnp.bfloat16):
    entries = jax.random.normal(key, shape, jnp.float32) * width
    if len(cuts) > 0:
        entries = level_of(key, shape, cuts, -0.22, 0.18) * entries
    return jnp.clip(entries, min=-reach, max=reach).astype(held_as)


def bell_draw_with(stream_key, shape, deviation, most, shards, heavy, kind=jnp.bfloat16):
    array = deviation * jax.random.normal(stream_key, shape, jnp.float32)
    if shards:
        array = array * level_of(stream_key, shape, shards, -0.22, 0.18)
    return jnp.clip(spiked(array, jax.random.fold_in(stream_key, 3), *heavy), -most, most).astype(kind)


def setup_inputs(seed: int = 0) -> dict:
    seeds = jax.random.split(jax.random.key(seed), 10)
    head_input = draw_head_input(jax.random.fold_in(seeds[9], 71), 0)
    gate_input = bell_draw(seeds[1], (SEQS, SEQLEN, INNER), 1.0, 5.0, ((0, 2), (1, 32), (2, 4)), jnp.float32)
    log_decay = draw_log_decay(jax.random.fold_in(seeds[9], 71), 0)
    in_b = bell_draw(seeds[3], (SEQS, SEQLEN, STATE), STATE ** -0.5, 0.5, ((0, 2), (1, 32)), jnp.float32)
    in_c = bell_draw(seeds[4], (SEQS, SEQLEN, STATE), (SEQLEN ** -0.5), 0.1875, ((0, 2), (1, 32)), jnp.float32)
    skip = jnp.clip(jnp.exp(math.log(2.0) - 1.3862944 * jax.random.uniform(seeds[5], (HEADS,), jnp.float32) ** level_of(seeds[5], (HEADS,), ((0, 4),), -0.2, 0.2)), 0.5, 2.0)
    norm_gain = jnp.clip(1.0 + 0.15 * jax.random.normal(seeds[6], (INNER,), jnp.float32), 0.25, 1.75)
    w_out = bell_draw(seeds[7], (INNER, D), INNER ** -0.5, 0.125, ((0, 4),), jnp.float32)
    d_out = bell_draw_with(seeds[8], (SEQS, SEQLEN, D), 1.0, 24.0, ((0, 2), (1, 128)), (1, 2, 128, 5.5), jnp.float32)
    return {"head_input": head_input, "gate_input": gate_input, "log_decay": log_decay, "in_b": in_b, "in_c": in_c, "skip": skip, "norm_gain": norm_gain, "w_out": w_out, "d_out": d_out}


highest = lax.Precision.HIGHEST

def ssd_output(x_heads, cum_decay, b_mat, c_mat, skip, state_in):
    length = x_heads.shape[0]
    causal = jnp.arange(length)[:, None] >= jnp.arange(length)[None, :]
    exponent = jnp.where(causal[None], cum_decay[:, :, None] - cum_decay[:, None, :], -1e+30)
    scores = jnp.dot(c_mat, b_mat.T, precision=highest)
    weights = jnp.exp(exponent) * scores[None]
    result = jnp.einsum('hts,shp->thp', weights, x_heads, precision=highest)
    carried = jnp.einsum('tn,hnp->thp', c_mat, state_in, precision=highest)
    result = result + carried * jnp.exp(cum_decay).T[:, :, None]
    return result + skip[None, :, None] * x_heads

def span_state(x_heads, cum_decay, b_mat):
    to_end = jnp.exp(cum_decay[:, -1:] - cum_decay)
    return jnp.einsum('sn,hs,shp->hnp', b_mat, to_end, x_heads, precision=highest)

def gate_norm(values, gate, gain):
    gated = values * jax.nn.silu(gate)
    rows = gated.shape[0]
    grouped = gated.reshape(rows, -1, GROUP)
    scale = lax.rsqrt(lax.optimization_barrier(jnp.mean(grouped * grouped, axis=2, keepdims=True)) + 1e-05)
    return (grouped * scale).reshape(rows, -1) * gain[None, :]

def reference(head_input, gate_input, log_decay, in_b, in_c, skip, norm_gain, w_out, d_out):

    def span_step(state, inputs):
        x_block, decay_block, b_block, c_block = inputs
        cum_decay = jnp.cumsum(decay_block, axis=1)
        y_block = ssd_output(x_block, cum_decay, b_block, c_block, skip, state)
        new_state = state * jnp.exp(cum_decay[:, -1])[:, None, None] + span_state(x_block, cum_decay, b_block)
        return (new_state, y_block)

    def forward(x_all, weight):
        results = []
        blocks = SEQLEN // TOK_DEV
        for sequence in range(SEQS):
            x_blocks = x_all[sequence].reshape(blocks, TOK_DEV, HEADS, HEAD)
            decay_blocks = log_decay[sequence].reshape(HEADS, blocks, TOK_DEV).transpose(1, 0, 2)
            b_blocks = in_b[sequence].reshape(blocks, TOK_DEV, STATE)
            c_blocks = in_c[sequence].reshape(blocks, TOK_DEV, STATE)
            start_state = jnp.zeros((HEADS, STATE, HEAD), jnp.float32)
            _, y_blocks = lax.scan(jax.checkpoint(span_step), start_state, (x_blocks, decay_blocks, b_blocks, c_blocks))
            y_flat = y_blocks.reshape(SEQLEN, HEADS * HEAD)
            normed = gate_norm(y_flat, gate_input[sequence], norm_gain)
            results.append(jnp.dot(normed, weight, precision=highest))
        return jnp.stack(results)
    out, pullback = jax.vjp(forward, head_input, w_out)
    grad_input, grad_w = pullback(d_out)
    return (out, grad_input, grad_w.T)
```

```python
import functools
import jax
import jax.numpy as jnp
from jax import lax
from jax.experimental import pallas as pl
from jax.experimental.pallas import tpu as pltpu
from jax.sharding import PartitionSpec as P

F32 = jnp.float32
BF16 = jnp.bfloat16
HEAD = 64
LANES = 128
EPS = 1e-05
NN = ((1,), (0,))
NT = ((1,), (1,))
TN = ((0,), (0,))
HIGHEST = lax.Precision.HIGHEST


def split(a):
    high = a.astype(BF16)
    return high, (a - high.astype(F32)).astype(BF16)


def dot(a, b, dims):
    return lax.dot_general(a, b, (dims, ((), ())), preferred_element_type=F32)


def dot3(a, b, dims):
    a_high, a_low = split(a)
    b_high, b_low = split(b)
    return dot(a_high, b_high, dims) + (dot(a_high, b_low, dims) + dot(a_low, b_high, dims))


def call(body, outs, ins, flops, nbytes, scratch=(), smem=(), grid=None, in_specs=None, out_specs=None, name=None):
    if in_specs is None:
        in_specs = [
            pl.BlockSpec(memory_space=pltpu.SMEM if i in smem else pltpu.VMEM) for i in range(len(ins))
        ]
        out_specs = [pl.BlockSpec(memory_space=pltpu.VMEM)] * len(outs)
    return pl.pallas_call(
        body,
        out_shape=[jax.ShapeDtypeStruct(s, F32) for s in outs],
        grid=grid if grid is not None else (),
        in_specs=in_specs,
        out_specs=out_specs,
        scratch_shapes=list(scratch),
        compiler_params=pltpu.CompilerParams(vmem_limit_bytes=48 * 1024 * 1024),
        cost_estimate=pl.CostEstimate(flops=flops, bytes_accessed=nbytes, transcendentals=0),
        name=name,
    )(*ins)


def pair(table, tile, rows, turned=False):
    lane = lax.broadcasted_iota(jnp.int32, (rows, LANES), 1)
    return jnp.where(lane < HEAD, table[:, 2 * tile : 2 * tile + 1], table[:, 2 * tile + 1 : 2 * tile + 2])


def pack(send_ref, state, ranks, pitch):
    rows = state.shape[0] // ranks
    for tile in range(state.shape[1] // LANES):
        for r in range(rows):
            send_ref[pl.ds(tile * rows + r, ranks, stride=pitch), :] = state[
                ranks * r : ranks * (r + 1), LANES * tile : LANES * (tile + 1)
            ]


def unpack(recv_ref, state_ref, ranks, pitch):
    rows = state_ref.shape[0] // ranks
    for tile in range(state_ref.shape[1] // LANES):
        for r in range(rows):
            state_ref[ranks * r : ranks * (r + 1), LANES * tile : LANES * (tile + 1)] = recv_ref[
                pl.ds(tile * rows + r, ranks, stride=pitch), :
            ]


def block_state(ranks, pitch, ld_ref, x_ref, b_ref, send_ref, cum_ref, cum_t_ref):
    length = x_ref.shape[0]
    row = lax.broadcasted_iota(jnp.int32, (length, length), 0)
    col = lax.broadcasted_iota(jnp.int32, (length, length), 1)
    upto = jnp.where(row >= col, 1.0, 0.0).astype(F32)
    ld = ld_ref[...]
    cum = lax.dot_general(ld, upto, (NT, ((), ())), precision=HIGHEST, preferred_element_type=F32)
    cum_t = lax.dot_general(upto, ld, (NT, ((), ())), precision=HIGHEST, preferred_element_type=F32)
    cum_ref[...] = cum
    cum_t_ref[...] = cum_t
    last = cum_t[length - 1 :, :]
    to_end = jnp.exp(last - cum_t)
    scaled = jnp.concatenate(
        [
            x_ref[:, LANES * tile : LANES * (tile + 1)] * pair(to_end, tile, length)
            for tile in range(x_ref.shape[1] // LANES)
        ],
        axis=1,
    )
    state = dot3(b_ref[...], scaled, TN)
    pack(send_ref, state, ranks, pitch)
    heads = ld.shape[0]
    totals = jnp.concatenate([last, jnp.zeros((1, LANES - heads), F32)], axis=1)
    totals = jnp.broadcast_to(totals, (ranks, LANES))
    used = state.size // ranks // LANES
    for spare in range(used, pitch):
        send_ref[pl.ds(spare, ranks, stride=pitch), :] = totals


def local_output(ld_heads, x_ref, b_ref, c_ref, cum_ref, cum_t_ref, skip_ref, y_ref):
    length = x_ref.shape[0]
    row = lax.broadcasted_iota(jnp.int32, (length, length), 0)
    col = lax.broadcasted_iota(jnp.int32, (length, length), 1)
    causal = row >= col
    scores = dot3(c_ref[...], b_ref[...], NT)
    cum = cum_ref[...]
    cum_t = cum_t_ref[...]
    for tile in range(ld_heads // 2):
        parts = []
        for head in (2 * tile, 2 * tile + 1):
            gap = jnp.where(causal, cum_t[:, head : head + 1] - cum[head : head + 1, :], -1e30)
            weights = jnp.exp(gap) * scores
            x = x_ref[:, HEAD * head : HEAD * (head + 1)]
            parts.append(dot3(weights, x, NN) + skip_ref[head] * x)
        y_ref[:, LANES * tile : LANES * (tile + 1)] = jnp.concatenate(parts, axis=1)


def local_grad(ld_heads, dy_ref, b_ref, c_ref, cum_ref, cum_t_ref, skip_ref, dx_ref):
    length = dy_ref.shape[0]
    row = lax.broadcasted_iota(jnp.int32, (length, length), 0)
    col = lax.broadcasted_iota(jnp.int32, (length, length), 1)
    causal = col >= row
    scores = dot3(b_ref[...], c_ref[...], NT)
    cum = cum_ref[...]
    cum_t = cum_t_ref[...]
    for tile in range(ld_heads // 2):
        parts = []
        for head in (2 * tile, 2 * tile + 1):
            gap = jnp.where(causal, cum[head : head + 1, :] - cum_t[:, head : head + 1], -1e30)
            weights = jnp.exp(gap) * scores
            dy = dy_ref[:, HEAD * head : HEAD * (head + 1)]
            parts.append(dot3(weights, dy, NN) + skip_ref[head] * dy)
        dx_ref[:, LANES * tile : LANES * (tile + 1)] = jnp.concatenate(parts, axis=1)


def scan_forward(ranks, pitch, used, width, recv_ref, send_ref, decay_ref):
    tiles = width // LANES
    rows = used // tiles
    totals = recv_ref[pl.ds(used, ranks, stride=pitch), :]
    decays = jnp.exp(totals)
    for tile in range(tiles):
        spread = pair(decays, tile, ranks)
        for r in range(rows):
            decay_ref[pl.ds(tile * rows + r, ranks, stride=pitch), :] = spread
    for spare in range(used, pitch):
        decay_ref[pl.ds(spare, ranks, stride=pitch), :] = decays
    state = jnp.zeros((pitch, LANES), F32)
    for rank in range(ranks):
        here = pl.ds(rank * pitch, pitch)
        send_ref[here, :] = state
        state = state * decay_ref[here, :] + recv_ref[here, :]


def scan_backward(ranks, pitch, recv_ref, decay_ref, send_ref):
    state = jnp.zeros((pitch, LANES), F32)
    for rank in reversed(range(ranks)):
        here = pl.ds(rank * pitch, pitch)
        send_ref[here, :] = state
        state = state * decay_ref[here, :] + recv_ref[here, :]


def gate_and_norm(ranks, pitch, recv_ref, c_ref, cum_t_ref, y_ref, gate_ref, gain_ref, gated_ref, normed_ref, scale_ref, state_ref):
    length, width = y_ref.shape
    unpack(recv_ref, state_ref, ranks, pitch)
    carried = dot3(c_ref[...], state_ref[...], NN)
    from_start = jnp.exp(cum_t_ref[...])
    total = jnp.zeros((length, LANES), F32)
    for tile in range(width // LANES):
        here = slice(LANES * tile, LANES * (tile + 1))
        y = y_ref[:, here] + carried[:, here] * pair(from_start, tile, length)
        gate = gate_ref[:, here]
        gated = y * (gate / (1.0 + jnp.exp(-gate)))
        gated_ref[:, here] = gated
        total = total + gated * gated
    scale = lax.rsqrt(jnp.sum(total, axis=1, keepdims=True) * (1.0 / width) + EPS)
    scale_ref[...] = jnp.broadcast_to(scale, scale_ref.shape)
    normed_ref[...] = gated_ref[...] * scale * gain_ref[...]


def out_blocks(ring, block, steps, pos_ref, normed_ref, w_ref, share_ref):
    half = pl.program_id(0) // (pl.num_programs(0) // 2)
    me = pos_ref[0]
    w = w_ref[...]
    rows = []
    for s in steps:
        index = lax.rem(jnp.where(half == 0, me + 2 * ring - 1 - s, me + 1 + s), ring)
        rows.append(normed_ref[pl.ds(pl.multiple_of(index * block, 8), block), :])
    product = dot3(jnp.concatenate(rows, axis=0) if len(rows) > 1 else rows[0], w, NN)
    for i in range(len(rows)):
        share_ref[i] = product[i * block : (i + 1) * block]


def d_normed_part(count, *refs):
    d_refs, w_ref, out_ref = refs[:count], refs[count], refs[count + 1]
    d = jnp.concatenate([r[...] for r in d_refs], axis=0) if count > 1 else d_refs[0][...]
    product = dot3(d, w_ref[...], NT)

    @pl.when(pl.program_id(0) == 0)
    def _():
        out_ref[...] = product

    @pl.when(pl.program_id(0) > 0)
    def _():
        out_ref[...] += product


def norm_grad(ranks, pitch, block, ring, pos_ref, near_ref, far_ref, gated_ref, scale_ref, gate_ref, gain_ref, c_ref, cum_t_ref, send_ref, dy_ref, dn_ref):
    length, width = gated_ref.shape
    me = pos_ref[0]
    order = ring_order(ring)
    for i, step in enumerate(order):
        index = lax.rem(me + step + ring, ring)
        src = near_ref[i * block : (i + 1) * block, :] if i < ring - 1 else far_ref[...]
        dn_ref[pl.ds(pl.multiple_of(index * block, 8), block), :] = src
    scale = scale_ref[:, :1]
    total = jnp.zeros((length, LANES), F32)
    for tile in range(width // LANES):
        here = slice(LANES * tile, LANES * (tile + 1))
        total = total + dn_ref[:, here] * gain_ref[:, here] * gated_ref[:, here]
    mean = jnp.sum(total, axis=1, keepdims=True) * (1.0 / width)
    shift = scale * scale * scale * mean
    from_start = jnp.exp(cum_t_ref[...])
    scaled = []
    for tile in range(width // LANES):
        here = slice(LANES * tile, LANES * (tile + 1))
        gate = gate_ref[:, here]
        d_gated = dn_ref[:, here] * gain_ref[:, here] * scale - gated_ref[:, here] * shift
        dy = d_gated * (gate / (1.0 + jnp.exp(-gate)))
        dy_ref[:, here] = dy
        scaled.append(dy * pair(from_start, tile, length))
    grad_state = dot3(c_ref[...], jnp.concatenate(scaled, axis=1), TN)
    pack(send_ref, grad_state, ranks, pitch)
    used = grad_state.size // ranks // LANES
    for spare in range(used, pitch):
        send_ref[pl.ds(spare, ranks, stride=pitch), :] = jnp.zeros((ranks, LANES), F32)


def ring_order(ring):
    return [0, -1, 1, 2]


def weight_grad(block, ring, pos_ref, d0_ref, d1_ref, d2_ref, d3_ref, normed_ref, out_ref):
    me = pos_ref[0]
    d = jnp.concatenate([d0_ref[...], d1_ref[...], d2_ref[...], d3_ref[...]], axis=0)
    rows = []
    for step in ring_order(ring):
        index = lax.rem(me + step + ring, ring)
        rows.append(normed_ref[pl.ds(pl.multiple_of(index * block, 8), block), :])
    out_ref[...] = dot3(d, jnp.concatenate(rows, axis=0), TN)


def finish(ranks, pitch, recv_ref, b_ref, cum_t_ref, part_ref, dx_ref, state_ref):
    length, width = part_ref.shape
    unpack(recv_ref, state_ref, ranks, pitch)
    carried = dot3(b_ref[...], state_ref[...], NN)
    cum_t = cum_t_ref[...]
    to_end = jnp.exp(cum_t[length - 1 :, :] - cum_t)
    for tile in range(width // LANES):
        here = slice(LANES * tile, LANES * (tile + 1))
        dx_ref[:, here] = part_ref[:, here] + carried[:, here] * pair(to_end, tile, length)


def shifted(value, axis, step):
    count = lax.axis_size(axis)
    return lax.ppermute(value, axis, [(i, (i + step) % count) for i in range(count)])


def exchange(value, axis):
    return lax.all_to_all(value, axis, 0, 0, tiled=True)


def per_device(head_input, gate_input, log_decay, in_b, in_c, skip, norm_gain, w_out, d_out):
    x, gate, ld, b_mat, c_mat, d_own = head_input[0], gate_input[0], log_decay[0], in_b[0], in_c[0], d_out[0]
    length, width = x.shape
    heads, state = ld.shape[0], b_mat.shape[1]
    model = w_out.shape[1]
    ranks, ring = lax.axis_size("ctx"), lax.axis_size("tp")
    block = d_own.shape[0]
    used = state * width // ranks // LANES
    pitch = -(-(used + 1) // 8) * 8
    gain = norm_gain[None, :]
    pos = lax.axis_index("tp").astype(jnp.int32)[None]
    half = model // 2

    d_prev = shifted(d_own, "tp", 1)
    d_next = shifted(d_own, "tp", -1)
    d_far = jnp.concatenate([shifted(d_prev[:, :half], "tp", 1), shifted(d_next[:, half:], "tp", -1)], axis=1)

    pieces = (ranks * pitch, LANES)
    send, cum, cum_t = call(
        functools.partial(block_state, ranks, pitch),
        [pieces, (heads, length), (length, heads)],
        [ld, x, b_mat],
        flops=6 * length * state * width, nbytes=4 * (length * width * 2), name="block_state",
    )
    recv = exchange(send, "ctx")
    (y_local,) = call(
        functools.partial(local_output, heads),
        [(length, width)],
        [x, b_mat, c_mat, cum, cum_t, skip],
        flops=6 * length * length * width * 4, nbytes=8 * length * width, smem=(5,), name="local_output",
    )
    send, decays = call(
        functools.partial(scan_forward, ranks, pitch, used, width),
        [pieces, pieces],
        [recv],
        flops=10 * ranks * pitch * LANES, nbytes=12 * ranks * pitch * LANES, name="scan_forward",
    )
    recv = exchange(send, "ctx")
    gated, normed, scale = call(
        functools.partial(gate_and_norm, ranks, pitch),
        [(length, width), (length, width), (length, LANES)],
        [recv, c_mat, cum_t, y_local, gate, gain],
        flops=6 * length * state * width, nbytes=16 * length * width,
        scratch=[pltpu.VMEM((state, width), F32)], name="gate_and_norm",
    )

    def out_part(steps):
        tile = 256
        return call(
            functools.partial(out_blocks, ring, block, steps),
            [(len(steps), block, model)],
            [pos, normed, w_out],
            flops=6 * len(steps) * block * width * model, nbytes=4 * width * model,
            grid=(model // tile,),
            in_specs=[
                pl.BlockSpec(memory_space=pltpu.SMEM),
                pl.BlockSpec((length, width), lambda n: (0, 0)),
                pl.BlockSpec((width, tile), lambda n: (0, n)),
            ],
            out_specs=[pl.BlockSpec((len(steps), block, tile), lambda n: (0, 0, n))],
            name="out_blocks",
        )[0]

    first = out_part((0,))[0]
    to_next, to_prev = first[:, :half], first[:, half:]
    rest = out_part(tuple(range(1, ring)))
    for s in range(ring - 1):
        to_next = shifted(to_next, "tp", 1) + rest[s][:, :half]
        to_prev = shifted(to_prev, "tp", -1) + rest[s][:, half:]
    out = jnp.concatenate([to_next, to_prev], axis=1)

    def d_part(parts):
        tile = 256
        rows = sum(p.shape[0] for p in parts)
        return call(
            functools.partial(d_normed_part, len(parts)),
            [(rows, width)],
            [*parts, w_out],
            flops=6 * rows * width * model, nbytes=4 * width * model,
            grid=(model // tile,),
            in_specs=[
                *[pl.BlockSpec((p.shape[0], tile), lambda k: (0, k)) for p in parts],
                pl.BlockSpec((width, tile), lambda k: (0, k)),
            ],
            out_specs=[pl.BlockSpec((rows, width), lambda k: (0, 0))],
            name="d_normed",
        )[0]

    near = d_part([d_own, d_prev, d_next])
    far = d_part([d_far])
    send, dy = call(
        functools.partial(norm_grad, ranks, pitch, block, ring),
        [pieces, (length, width)],
        [pos, near, far, gated, scale, gate, gain, c_mat, cum_t],
        flops=6 * length * state * width, nbytes=20 * length * width, smem=(0,),
        scratch=[pltpu.VMEM((length, width), F32)], name="norm_grad",
    )
    recv = exchange(send, "ctx")
    tile = 256
    (grad_w,) = call(
        functools.partial(weight_grad, block, ring),
        [(model, width)],
        [pos, d_own, d_prev, d_next, d_far, normed],
        flops=6 * length * width * model, nbytes=4 * width * model,
        grid=(model // tile,),
        in_specs=[
            pl.BlockSpec(memory_space=pltpu.SMEM),
            *[pl.BlockSpec((block, tile), lambda k: (0, k))] * 4,
            pl.BlockSpec((length, width), lambda k: (0, 0)),
        ],
        out_specs=[pl.BlockSpec((tile, width), lambda k: (k, 0))],
        name="weight_grad",
    )
    grad_share = lax.psum_scatter(
        lax.psum_scatter(grad_w, "ctx", scatter_dimension=0, tiled=True), "dp", scatter_dimension=0, tiled=True
    )
    (dx_local,) = call(
        functools.partial(local_grad, heads),
        [(length, width)],
        [dy, b_mat, c_mat, cum, cum_t, skip],
        flops=6 * length * length * width * 4, nbytes=8 * length * width, smem=(5,), name="local_grad",
    )
    (send,) = call(
        functools.partial(scan_backward, ranks, pitch),
        [pieces],
        [recv, decays],
        flops=10 * ranks * pitch * LANES, nbytes=12 * ranks * pitch * LANES, name="scan_backward",
    )
    recv = exchange(send, "ctx")
    (dx,) = call(
        functools.partial(finish, ranks, pitch),
        [(length, width)],
        [recv, b_mat, cum_t, dx_local],
        flops=6 * length * state * width, nbytes=12 * length * width,
        scratch=[pltpu.VMEM((state, width), F32)], name="finish",
    )
    return (out[None], dx[None], grad_share)


def solution(mesh):
    placed = (
        P("dp", "ctx", "tp"),
        P("dp", "ctx", "tp"),
        P("dp", "tp", "ctx"),
        P("dp", "ctx", None),
        P("dp", "ctx", None),
        P("tp"),
        P("tp"),
        P("tp", None),
        P("dp", ("ctx", "tp"), None),
    )
    return jax.shard_map(
        per_device,
        mesh=mesh,
        in_specs=placed,
        out_specs=(P("dp", ("ctx", "tp"), None), P("dp", "ctx", "tp"), P(("ctx", "dp"), "tp")),
        check_vma=False,
    )
```

```python
import functools
import jax
import jax.numpy as jnp
from jax import lax
from jax.experimental import pallas as pl
from jax.experimental.pallas import tpu as pltpu
from jax.sharding import PartitionSpec as P

F32 = jnp.float32
BF16 = jnp.bfloat16
HEAD = 64
LANES = 128
EPS = 1e-05
NN = ((1,), (0,))
NT = ((1,), (1,))
TN = ((0,), (0,))
HIGHEST = lax.Precision.HIGHEST


def split(a):
    high = a.astype(BF16)
    return high, (a - high.astype(F32)).astype(BF16)


def dot(a, b, dims):
    return lax.dot_general(a, b, (dims, ((), ())), preferred_element_type=F32)


def dot3(a, b, dims):
    a_high, a_low = split(a)
    b_high, b_low = split(b)
    return dot(a_high, b_high, dims) + (dot(a_high, b_low, dims) + dot(a_low, b_high, dims))


TILE = 256


class Copies:
    def __init__(self, sources, held, in_sems, tile_sems, made, targets, out_sems):
        self.sources, self.held, self.in_sems, self.tile_sems = sources, held, in_sems, tile_sems
        self.out = [pltpu.make_async_copy(a, b, out_sems.at[j]) for j, (a, b) in enumerate(zip(made, targets))]
        self.started = set()

    def whole(self, i):
        return pltpu.make_async_copy(self.sources[i], self.held[i], self.in_sems.at[i])

    def tile(self, i, k):
        here = pl.ds(pl.multiple_of(k * TILE, TILE), TILE)
        return pltpu.make_async_copy(self.sources[i].at[:, here], self.held[i].at[:, here], self.tile_sems.at[k])

    def flush(self, *which):
        for j in which:
            self.out[j].start()
            self.started.add(j)


def call(body, outs, ins, name, us, scratch=(), smem=(), tiled=None, after=(), io=False, fixed=(), vmem=40):
    outs = [o if isinstance(o, jax.ShapeDtypeStruct) else jax.ShapeDtypeStruct(o, F32) for o in outs]
    n, m = len(ins), len(outs)
    big = [i for i in range(n) if i not in smem]
    tiles = ins[tiled].shape[1] // TILE if tiled is not None else 1

    def run(*refs):
        refs = list(refs)
        sources, refs = refs[:n], refs[n + len(after) :]
        targets, refs = refs[:m], refs[m:]
        held, refs = dict(zip(big, refs[: len(big)])), refs[len(big) :]
        made, refs = refs[:m], refs[m:]
        in_sems, tile_sems, out_sems = refs[:3]
        copies = Copies(sources, held, in_sems, tile_sems, made, targets, out_sems)
        for i in big:
            if i != tiled:
                copies.whole(i).start()
        if tiled is not None:
            for k in range(tiles):
                copies.tile(tiled, k).start()
        for i in big:
            if i != tiled:
                copies.whole(i).wait()
        operands = [held.get(i, sources[i]) for i in range(n)]
        body(*([copies] if io else []), *operands, *made, *refs[3:])
        copies.flush(*[j for j in range(m) if j not in copies.started])
        for c in copies.out:
            c.wait()

    return pl.pallas_call(
        run,
        out_shape=outs,
        in_specs=[
            *[pl.BlockSpec(memory_space=pltpu.SMEM if i in smem else pltpu.HBM) for i in range(n)],
            *[pl.BlockSpec(memory_space=pltpu.HBM)] * len(after),
        ],
        out_specs=[pl.BlockSpec(memory_space=pltpu.HBM)] * m,
        scratch_shapes=[
            *[pltpu.VMEM(ins[i].shape, ins[i].dtype) for i in big],
            *[pltpu.VMEM(o.shape, o.dtype) for o in outs],
            pltpu.SemaphoreType.DMA((n,)),
            pltpu.SemaphoreType.DMA((tiles,)),
            pltpu.SemaphoreType.DMA((m,)),
            *scratch,
        ],
        compiler_params=pltpu.CompilerParams(vmem_limit_bytes=vmem * 1024 * 1024),
        cost_estimate=pl.CostEstimate(flops=0, bytes_accessed=int(us * 3e6), transcendentals=0),
        name=name,
    )(*[pltpu.with_memory_space_constraint(v, pltpu.HBM) if i in fixed else v for i, v in enumerate(ins)], *after)


def pair(table, tile, rows, turned=False):
    lane = lax.broadcasted_iota(jnp.int32, (rows, LANES), 1)
    return jnp.where(lane < HEAD, table[:, 2 * tile : 2 * tile + 1], table[:, 2 * tile + 1 : 2 * tile + 2])


def pack(send_ref, state, ranks, pitch):
    rows = state.shape[0] // ranks
    for tile in range(state.shape[1] // LANES):
        for r in range(rows):
            send_ref[pl.ds(tile * rows + r, ranks, stride=pitch), :] = state[
                ranks * r : ranks * (r + 1), LANES * tile : LANES * (tile + 1)
            ]


def unpack(recv_ref, state_ref, ranks, pitch):
    rows = state_ref.shape[0] // ranks
    for tile in range(state_ref.shape[1] // LANES):
        for r in range(rows):
            state_ref[ranks * r : ranks * (r + 1), LANES * tile : LANES * (tile + 1)] = recv_ref[
                pl.ds(tile * rows + r, ranks, stride=pitch), :
            ]


def block_state(ranks, pitch, ld_ref, x_ref, b_ref, send_ref, cum_ref, cum_t_ref):
    length = x_ref.shape[0]
    row = lax.broadcasted_iota(jnp.int32, (length, length), 0)
    col = lax.broadcasted_iota(jnp.int32, (length, length), 1)
    upto = jnp.where(row >= col, 1.0, 0.0).astype(F32)
    ld = ld_ref[...]
    cum = lax.dot_general(ld, upto, (NT, ((), ())), precision=HIGHEST, preferred_element_type=F32)
    cum_t = lax.dot_general(upto, ld, (NT, ((), ())), precision=HIGHEST, preferred_element_type=F32)
    cum_ref[...] = cum
    cum_t_ref[...] = cum_t
    last = cum_t[length - 1 :, :]
    to_end = jnp.exp(last - cum_t)
    scaled = jnp.concatenate(
        [
            x_ref[:, LANES * tile : LANES * (tile + 1)] * pair(to_end, tile, length)
            for tile in range(x_ref.shape[1] // LANES)
        ],
        axis=1,
    )
    state = dot3(b_ref[...], scaled, TN)
    pack(send_ref, state, ranks, pitch)
    heads = ld.shape[0]
    totals = jnp.concatenate([last, jnp.zeros((1, LANES - heads), F32)], axis=1)
    totals = jnp.broadcast_to(totals, (ranks, LANES))
    used = state.size // ranks // LANES
    for spare in range(used, pitch):
        send_ref[pl.ds(spare, ranks, stride=pitch), :] = totals


def local_output(ld_heads, x_ref, b_ref, c_ref, cum_ref, cum_t_ref, skip_ref, y_ref):
    length = x_ref.shape[0]
    row = lax.broadcasted_iota(jnp.int32, (length, length), 0)
    col = lax.broadcasted_iota(jnp.int32, (length, length), 1)
    causal = row >= col
    scores = dot3(c_ref[...], b_ref[...], NT)
    cum = cum_ref[...]
    cum_t = cum_t_ref[...]
    for tile in range(ld_heads // 2):
        parts = []
        for head in (2 * tile, 2 * tile + 1):
            gap = jnp.where(causal, cum_t[:, head : head + 1] - cum[head : head + 1, :], -1e30)
            weights = jnp.exp(gap) * scores
            x = x_ref[:, HEAD * head : HEAD * (head + 1)]
            parts.append(dot3(weights, x, NN) + skip_ref[head] * x)
        y_ref[:, LANES * tile : LANES * (tile + 1)] = jnp.concatenate(parts, axis=1)


def local_grad(ld_heads, dy_ref, b_ref, c_ref, cum_ref, cum_t_ref, skip_ref, dx_ref):
    length = dy_ref.shape[0]
    row = lax.broadcasted_iota(jnp.int32, (length, length), 0)
    col = lax.broadcasted_iota(jnp.int32, (length, length), 1)
    causal = col >= row
    scores = dot3(b_ref[...], c_ref[...], NT)
    cum = cum_ref[...]
    cum_t = cum_t_ref[...]
    for tile in range(ld_heads // 2):
        parts = []
        for head in (2 * tile, 2 * tile + 1):
            gap = jnp.where(causal, cum[head : head + 1, :] - cum_t[:, head : head + 1], -1e30)
            weights = jnp.exp(gap) * scores
            dy = dy_ref[:, HEAD * head : HEAD * (head + 1)]
            parts.append(dot3(weights, dy, NN) + skip_ref[head] * dy)
        dx_ref[:, LANES * tile : LANES * (tile + 1)] = jnp.concatenate(parts, axis=1)


def scan_forward(ranks, pitch, used, width, recv_ref, send_ref, decay_ref):
    tiles = width // LANES
    rows = used // tiles
    totals = recv_ref[pl.ds(used, ranks, stride=pitch), :]
    decays = jnp.exp(totals)
    for tile in range(tiles):
        spread = pair(decays, tile, ranks)
        for r in range(rows):
            decay_ref[pl.ds(tile * rows + r, ranks, stride=pitch), :] = spread
    for spare in range(used, pitch):
        decay_ref[pl.ds(spare, ranks, stride=pitch), :] = decays
    state = jnp.zeros((pitch, LANES), F32)
    for rank in range(ranks):
        here = pl.ds(rank * pitch, pitch)
        send_ref[here, :] = state
        state = state * decay_ref[here, :] + recv_ref[here, :]


def scan_backward(ranks, pitch, recv_ref, decay_ref, send_ref):
    state = jnp.zeros((pitch, LANES), F32)
    for rank in reversed(range(ranks)):
        here = pl.ds(rank * pitch, pitch)
        send_ref[here, :] = state
        state = state * decay_ref[here, :] + recv_ref[here, :]


def gate_out(
    ring, ranks, pitch, io, pos_ref, recv_ref, c_ref, cum_t_ref, y_ref, gate_ref, gain_ref, w_ref,
    gated_ref, normed_ref, scale_ref, far_left_ref, far_right_ref, next_ref, prev_ref, own_ref,
    state_ref, high_ref, low_ref,
):
    length, width = y_ref.shape
    unpack(recv_ref, state_ref, ranks, pitch)
    carried = dot3(c_ref[...], state_ref[...], NN)
    from_start = jnp.exp(cum_t_ref[...])
    total = jnp.zeros((length, LANES), F32)
    for tile in range(width // LANES):
        here = slice(LANES * tile, LANES * (tile + 1))
        y = y_ref[:, here] + carried[:, here] * pair(from_start, tile, length)
        gate = gate_ref[:, here]
        gated = y * (gate / (1.0 + jnp.exp(-gate)))
        gated_ref[:, here] = gated
        total = total + gated * gated
    scale = lax.rsqrt(jnp.sum(total, axis=1, keepdims=True) * (1.0 / width) + EPS)
    scale_ref[...] = jnp.broadcast_to(scale, scale_ref.shape)
    normed_ref[...] = gated_ref[...] * scale * gain_ref[...]
    io.flush(0, 1, 2)
    me = pos_ref[0]
    block = own_ref.shape[0]
    rows = []
    for step in (2, 1, -1, 0):
        index = lax.rem(me + step + ring, ring)
        rows.append(normed_ref[pl.ds(pl.multiple_of(index * block, 8), block), :])
    high_ref[...], low_ref[...] = split(jnp.concatenate(rows, axis=0))
    half = far_left_ref.shape[1]
    for side, far_ref in enumerate((far_left_ref, far_right_ref)):

        @pl.loop(0, half // TILE)
        def _(n):
            k = side * (half // TILE) + n
            io.tile(7, k).wait()
            here = pl.ds(pl.multiple_of(k * TILE, TILE), TILE)
            high, low = split(w_ref[:, here])
            product = dot(high_ref[...], high, NN) + (dot(high_ref[...], low, NN) + dot(low_ref[...], high, NN))
            far_ref[:, pl.ds(pl.multiple_of(n * TILE, TILE), TILE)] = product[:block]
            next_ref[:, here] = product[block : 2 * block]
            prev_ref[:, here] = product[2 * block : 3 * block]
            own_ref[:, here] = product[3 * block :]

        io.flush(3 + side)


def turn(
    ring, rows, pos_ref, own_ref, prev_ref, next_ref, far_left_ref, far_right_ref, normed_ref,
    keep_ref, give_ref, high_ref, low_ref, held_ref, turned_ref,
):
    me, core = pos_ref[0], pos_ref[1]
    block, model = own_ref.shape
    length = normed_ref.shape[0]
    wide, padded = turned_ref.shape
    held_ref[length:, :] = jnp.zeros((padded - length, wide), F32)
    for part in range(model // wide):
        here = slice(part * wide, (part + 1) * wide)
        if part * wide < model // 2:
            far = far_left_ref[:, here]
        else:
            far = far_right_ref[:, part * wide - model // 2 : (part + 1) * wide - model // 2]
        for step, piece in ((0, own_ref[:, here]), (-1, prev_ref[:, here]), (1, next_ref[:, here]), (2, far)):
            index = lax.rem(me + step + ring, ring)
            held_ref[pl.ds(pl.multiple_of(index * block, 8), block), :] = piece
        turned = held_ref[...].T
        turned_ref[...] = turned
        high_ref[here, :], low_ref[here, :] = split(turned)
        for chip in range(wide // (2 * rows)):
            at = (part * wide // (2 * rows) + chip) * rows
            keep_ref[at : at + rows, :] = turned_ref[pl.ds(pl.multiple_of((2 * chip + core) * rows, 8), rows), :]
            give_ref[at : at + rows, :] = turned_ref[pl.ds(pl.multiple_of((2 * chip + 1 - core) * rows, 8), rows), :]
    width = normed_ref.shape[1]
    held_ref[:length, :width] = normed_ref[...]
    give_ref[model // 2 :, :] = held_ref[:, :width].T


def normed_grad(io, high_ref, low_ref, w_ref, dn_ref, sum_ref):
    sum_ref[...] = jnp.zeros_like(sum_ref)

    @pl.loop(0, w_ref.shape[1] // TILE)
    def _(k):
        io.tile(2, k).wait()
        here = pl.ds(pl.multiple_of(k * TILE, TILE), TILE)
        w_high, w_low = split(w_ref[:, here])
        high, low = high_ref[here, :], low_ref[here, :]
        sum_ref[...] += dot(w_high, high, NN) + (dot(w_high, low, NN) + dot(w_low, high, NN))

    dn_ref[...] = sum_ref[...].T[: dn_ref.shape[0]]


def norm_grad(
    ranks, pitch, dn_ref, gated_ref, scale_ref, gate_ref, gain_ref, c_ref, cum_t_ref, send_ref, dy_ref
):
    length, width = gated_ref.shape
    scale = scale_ref[:, :1]
    total = jnp.zeros((length, LANES), F32)
    for tile in range(width // LANES):
        here = slice(LANES * tile, LANES * (tile + 1))
        total = total + dn_ref[:, here] * gain_ref[:, here] * gated_ref[:, here]
    mean = jnp.sum(total, axis=1, keepdims=True) * (1.0 / width)
    shift = scale * scale * scale * mean
    from_start = jnp.exp(cum_t_ref[...])
    scaled = []
    for tile in range(width // LANES):
        here = slice(LANES * tile, LANES * (tile + 1))
        gate = gate_ref[:, here]
        d_gated = dn_ref[:, here] * gain_ref[:, here] * scale - gated_ref[:, here] * shift
        dy = d_gated * (gate / (1.0 + jnp.exp(-gate)))
        dy_ref[:, here] = dy
        scaled.append(dy * pair(from_start, tile, length))
    grad_state = dot3(c_ref[...], jnp.concatenate(scaled, axis=1), TN)
    pack(send_ref, grad_state, ranks, pitch)
    used = grad_state.size // ranks // LANES
    for spare in range(used, pitch):
        send_ref[pl.ds(spare, ranks, stride=pitch), :] = jnp.zeros((ranks, LANES), F32)


def weight_grad(across, down, io, keep_ref, other_ref, normed_ref, out_ref, n_high_ref, n_low_ref, o_high_ref, o_low_ref):
    length, width = normed_ref.shape
    padded = keep_ref.shape[1]
    rows = keep_ref.shape[0] // (across * down)
    n_high_ref[:length, :], n_low_ref[:length, :] = split(normed_ref[...])
    n_high_ref[length:, :] = jnp.zeros((padded - length, width), BF16)
    n_low_ref[length:, :] = jnp.zeros((padded - length, width), BF16)
    o_high_ref[...], o_low_ref[...] = split(other_ref[keep_ref.shape[0] :, :].T)
    n_high, n_low, o_high, o_low = n_high_ref[...], n_low_ref[...], o_high_ref[...], o_low_ref[...]
    for y in range(down):
        here = slice(y * across * rows, (y + 1) * across * rows)
        k_high, k_low = split(keep_ref[here, :])
        t_high, t_low = split(other_ref[here, :])
        small = dot(k_high, n_low, NN) + dot(k_low, n_high, NN) + dot(t_high, o_low, NN) + dot(t_low, o_high, NN)
        product = dot(k_high, n_high, NN) + dot(t_high, o_high, NN) + small
        for x in range(across):
            at = (x * down + y) * rows
            out_ref[at : at + rows, :] = product[x * rows : (x + 1) * rows]


def sum_column(count, recv_ref, share_ref):
    rows = share_ref.shape[0]
    total = recv_ref[:rows, :]
    for i in range(1, count):
        total = total + recv_ref[i * rows : (i + 1) * rows, :]
    share_ref[...] = total


def pass_on(next_ref, prev_ref, up_ref, down_ref, next_out_ref, prev_out_ref):
    half = up_ref.shape[1]
    next_out_ref[:, :half] = next_ref[:, :half] + up_ref[...]
    next_out_ref[:, half:] = next_ref[:, half:]
    prev_out_ref[:, :half] = prev_ref[:, :half]
    prev_out_ref[:, half:] = prev_ref[:, half:] + down_ref[...]


def finish(ranks, pitch, recv_ref, b_ref, cum_t_ref, part_ref, dx_ref, state_ref):
    length, width = part_ref.shape
    unpack(recv_ref, state_ref, ranks, pitch)
    carried = dot3(b_ref[...], state_ref[...], NN)
    cum_t = cum_t_ref[...]
    to_end = jnp.exp(cum_t[length - 1 :, :] - cum_t)
    for tile in range(width // LANES):
        here = slice(LANES * tile, LANES * (tile + 1))
        dx_ref[:, here] = part_ref[:, here] + carried[:, here] * pair(to_end, tile, length)


def shifted(value, axis, step):
    count = lax.axis_size(axis)
    return lax.ppermute(value, axis, [(i, (i + step) % count) for i in range(count)])


def swapped(value, axis):
    return lax.ppermute(value, axis, [(i, i ^ 1) for i in range(lax.axis_size(axis))])


def exchange(value, axis):
    return lax.all_to_all(value, axis, 0, 0, tiled=True)


def per_device(head_input, gate_input, log_decay, in_b, in_c, skip, norm_gain, w_out, d_out):
    x, gate, ld, b_mat, c_mat, d_own = head_input[0], gate_input[0], log_decay[0], in_b[0], in_c[0], d_out[0]
    length, width = x.shape
    heads, state = ld.shape[0], b_mat.shape[1]
    model = w_out.shape[1]
    ranks, ring, seqs = lax.axis_size("ctx"), lax.axis_size("tp"), lax.axis_size("dp")
    block = d_own.shape[0]
    used = state * width // ranks // LANES
    pitch = -(-(used + 1) // 8) * 8
    pieces = (ranks * pitch, LANES)
    gain = norm_gain[None, :]
    dp = lax.axis_index("dp")
    pos = jnp.stack([lax.axis_index("tp"), lax.rem(lax.axis_index("ctx"), 2), dp]).astype(jnp.int32)
    half = model // 2
    chips = ranks // 2
    rows = model // ranks
    wide = max(width, 2 * rows)
    padded = -(-length // LANES) * LANES
    across = 4 if chips % 16 == 0 else 2
    down = chips // across
    lines = [[y * across + x for x in range(across)] for y in range(down)]
    lines = [
        [[2 * chip + c for chip in line] for line in way for c in range(2)] for way in (lines, list(zip(*lines)))
    ]

    d_prev, d_next = shifted(d_own, "tp", 1), shifted(d_own, "tp", -1)
    far_left, far_right = shifted(d_prev[:, :half], "tp", 1), shifted(d_next[:, half:], "tp", -1)

    send, cum, cum_t = call(
        functools.partial(block_state, ranks, pitch),
        [pieces, (heads, length), (length, heads)],
        [ld, x, b_mat],
        fixed=(0, 1, 2), name="block_state", us=0.3,
    )
    recv = exchange(send, "ctx")
    (y_local,) = call(
        functools.partial(local_output, heads),
        [(length, width)],
        [x, b_mat, c_mat, cum, cum_t, skip],
        smem=(5,), fixed=(0, 1, 2), name="local_output", us=0.3,
    )
    send, decays = call(
        functools.partial(scan_forward, ranks, pitch, used, width),
        [pieces, pieces],
        [recv],
        after=[y_local], name="scan_forward", us=0.3,
    )
    recv = exchange(send, "ctx")
    gated, normed, scale, part_left, part_right, part_next, part_prev, part_own = call(
        functools.partial(gate_out, ring, ranks, pitch),
        [(length, width)] * 2 + [(length, LANES)] + [(block, half)] * 2 + [(block, model)] * 3,
        [pos, recv, c_mat, cum_t, y_local, gate, gain, w_out],
        smem=(0,), tiled=7, fixed=(2, 5, 7), io=True,
        scratch=[pltpu.VMEM((state, width), F32)] + [pltpu.VMEM((length, width), BF16)] * 2,
        name="gate_out", us=7,
    )
    up_far, down_far = shifted(part_left, "tp", 1), shifted(part_right, "tp", -1)
    keep, give, d_high, d_low = call(
        functools.partial(turn, ring, rows),
        [(half, padded), (half + width, padded)] + [jax.ShapeDtypeStruct((model, padded), BF16)] * 2,
        [pos, d_own, d_prev, d_next, far_left, far_right, normed],
        scratch=[pltpu.VMEM((padded, wide), F32), pltpu.VMEM((wide, padded), F32)],
        smem=(0,), name="turn", us=0.3,
    )
    other = swapped(give, "ctx")
    (d_normed,) = call(
        normed_grad, [(length, width)], [d_high, d_low, w_out],
        tiled=2, fixed=(2,), io=True, scratch=[pltpu.VMEM((width, padded), F32)], name="normed_grad", us=0.3,
    )
    (grad_w,) = call(
        functools.partial(weight_grad, across, down), [(half, width)], [keep, other, normed],
        scratch=[pltpu.VMEM((padded, width), BF16)] * 4,
        io=True, after=[d_normed], name="weight_grad", us=0.3,
    )
    grad_w = lax.psum_scatter(grad_w, "ctx", scatter_dimension=0, tiled=True, axis_index_groups=lines[0])
    send, dy = call(
        functools.partial(norm_grad, ranks, pitch),
        [pieces, (length, width)],
        [d_normed, gated, scale, gate, gain, c_mat, cum_t],
        fixed=(3,), name="norm_grad", us=0.3,
    )
    recv = exchange(send, "ctx")
    (dx_local,) = call(
        functools.partial(local_grad, heads),
        [(length, width)],
        [dy, b_mat, c_mat, cum, cum_t, skip],
        smem=(5,), fixed=(1, 2), name="local_grad", us=0.3,
    )
    part_next, part_prev = call(
        pass_on, [(block, model)] * 2, [part_next, part_prev, up_far, down_far],
        after=[dx_local], name="pass_on", us=0.3,
    )
    up, low = shifted(part_next, "tp", 1), shifted(part_prev, "tp", -1)
    (send,) = call(
        functools.partial(scan_backward, ranks, pitch),
        [pieces],
        [recv, decays],
        after=[part_next], name="scan_backward", us=0.3,
    )
    recv = exchange(send, "ctx")
    (dx,) = call(
        functools.partial(finish, ranks, pitch),
        [(length, width)],
        [recv, b_mat, cum_t, dx_local],
        fixed=(1,),
        scratch=[pltpu.VMEM((state, width), F32)], name="finish", us=0.3,
    )
    out = part_own + up + low
    grad_w, _, out = lax.optimization_barrier((grad_w, dx, out))
    columns = [[seqs * i + p for i in line for p in range(seqs)] for line in lines[1]]
    grad_w = lax.all_to_all(grad_w, ("ctx", "dp"), 0, 0, tiled=True, axis_index_groups=columns)
    (share,) = call(
        functools.partial(sum_column, down * seqs), [(rows // seqs, width)], [grad_w],
        name="sum_column", us=1,
    )
    return (out[None], dx[None], share)


def solution(mesh):
    placed = (
        P("dp", "ctx", "tp"),
        P("dp", "ctx", "tp"),
        P("dp", "tp", "ctx"),
        P("dp", "ctx", None),
        P("dp", "ctx", None),
        P("tp"),
        P("tp"),
        P("tp", None),
        P("dp", ("ctx", "tp"), None),
    )
    return jax.shard_map(
        per_device,
        mesh=mesh,
        in_specs=placed,
        out_specs=(P("dp", ("ctx", "tp"), None), P("dp", "ctx", "tp"), P(("ctx", "dp"), "tp")),
        check_vma=False,
    )
```

```python
import functools
import jax
import jax.numpy as jnp
from jax import lax
from jax.experimental import pallas as pl
from jax.experimental.pallas import tpu as pltpu
from jax.sharding import PartitionSpec as P

F32 = jnp.float32
BF16 = jnp.bfloat16
HEAD = 64
LANES = 128
EPS = 1e-05
NN = ((1,), (0,))
NT = ((1,), (1,))
TN = ((0,), (0,))
HIGHEST = lax.Precision.HIGHEST


def split(a):
    high = a.astype(BF16)
    return high, (a - high.astype(F32)).astype(BF16)


def dot(a, b, dims):
    return lax.dot_general(a, b, (dims, ((), ())), preferred_element_type=F32)


def dot3(a, b, dims):
    a_high, a_low = split(a)
    b_high, b_low = split(b)
    return dot(a_high, b_high, dims) + (dot(a_high, b_low, dims) + dot(a_low, b_high, dims))


TILE = 256


class Copies:
    def __init__(self, sources, held, in_sems, tile_sems, made, targets, out_sems):
        self.sources, self.held, self.in_sems, self.tile_sems = sources, held, in_sems, tile_sems
        self.out = [pltpu.make_async_copy(a, b, out_sems.at[j]) for j, (a, b) in enumerate(zip(made, targets))]
        self.started = set()

    def whole(self, i):
        return pltpu.make_async_copy(self.sources[i], self.held[i], self.in_sems.at[i])

    def tile(self, i, k):
        here = pl.ds(pl.multiple_of(k * TILE, TILE), TILE)
        return pltpu.make_async_copy(self.sources[i].at[:, here], self.held[i].at[:, here], self.tile_sems.at[k])

    def flush(self, *which):
        for j in which:
            self.out[j].start()
            self.started.add(j)


def call(body, outs, ins, name, us, scratch=(), smem=(), tiled=None, after=(), io=False, fixed=(), vmem=40):
    outs = [o if isinstance(o, jax.ShapeDtypeStruct) else jax.ShapeDtypeStruct(o, F32) for o in outs]
    n, m = len(ins), len(outs)
    big = [i for i in range(n) if i not in smem]
    tiles = ins[tiled].shape[1] // TILE if tiled is not None else 1

    def run(*refs):
        refs = list(refs)
        sources, refs = refs[:n], refs[n + len(after) :]
        targets, refs = refs[:m], refs[m:]
        held, refs = dict(zip(big, refs[: len(big)])), refs[len(big) :]
        made, refs = refs[:m], refs[m:]
        in_sems, tile_sems, out_sems = refs[:3]
        copies = Copies(sources, held, in_sems, tile_sems, made, targets, out_sems)
        for i in big:
            if i != tiled:
                copies.whole(i).start()
        if tiled is not None:
            for k in range(tiles):
                copies.tile(tiled, k).start()
        for i in big:
            if i != tiled:
                copies.whole(i).wait()
        operands = [held.get(i, sources[i]) for i in range(n)]
        body(*([copies] if io else []), *operands, *made, *refs[3:])
        copies.flush(*[j for j in range(m) if j not in copies.started])
        for c in copies.out:
            c.wait()

    return pl.pallas_call(
        run,
        out_shape=outs,
        in_specs=[
            *[pl.BlockSpec(memory_space=pltpu.SMEM if i in smem else pltpu.HBM) for i in range(n)],
            *[pl.BlockSpec(memory_space=pltpu.HBM)] * len(after),
        ],
        out_specs=[pl.BlockSpec(memory_space=pltpu.HBM)] * m,
        scratch_shapes=[
            *[pltpu.VMEM(ins[i].shape, ins[i].dtype) for i in big],
            *[pltpu.VMEM(o.shape, o.dtype) for o in outs],
            pltpu.SemaphoreType.DMA((n,)),
            pltpu.SemaphoreType.DMA((tiles,)),
            pltpu.SemaphoreType.DMA((m,)),
            *scratch,
        ],
        compiler_params=pltpu.CompilerParams(vmem_limit_bytes=vmem * 1024 * 1024),
        cost_estimate=pl.CostEstimate(flops=0, bytes_accessed=int(us * 3e6), transcendentals=0),
        name=name,
    )(*[pltpu.with_memory_space_constraint(v, pltpu.HBM) if i in fixed else v for i, v in enumerate(ins)], *after)


def pair(table, tile, rows, turned=False):
    lane = lax.broadcasted_iota(jnp.int32, (rows, LANES), 1)
    return jnp.where(lane < HEAD, table[:, 2 * tile : 2 * tile + 1], table[:, 2 * tile + 1 : 2 * tile + 2])


def pack(send_ref, state, ranks, pitch):
    rows = state.shape[0] // ranks
    for tile in range(state.shape[1] // LANES):
        for r in range(rows):
            send_ref[pl.ds(tile * rows + r, ranks, stride=pitch), :] = state[
                ranks * r : ranks * (r + 1), LANES * tile : LANES * (tile + 1)
            ]


def unpack(recv_ref, state_ref, ranks, pitch):
    rows = state_ref.shape[0] // ranks
    for tile in range(state_ref.shape[1] // LANES):
        for r in range(rows):
            state_ref[ranks * r : ranks * (r + 1), LANES * tile : LANES * (tile + 1)] = recv_ref[
                pl.ds(tile * rows + r, ranks, stride=pitch), :
            ]


def block_state(ranks, pitch, ld_ref, x_ref, b_ref, send_ref, cum_ref, cum_t_ref):
    length = x_ref.shape[0]
    row = lax.broadcasted_iota(jnp.int32, (length, length), 0)
    col = lax.broadcasted_iota(jnp.int32, (length, length), 1)
    upto = jnp.where(row >= col, 1.0, 0.0).astype(F32)
    ld = ld_ref[...]
    cum = lax.dot_general(ld, upto, (NT, ((), ())), precision=HIGHEST, preferred_element_type=F32)
    cum_t = lax.dot_general(upto, ld, (NT, ((), ())), precision=HIGHEST, preferred_element_type=F32)
    cum_ref[...] = cum
    cum_t_ref[...] = cum_t
    last = cum_t[length - 1 :, :]
    to_end = jnp.exp(last - cum_t)
    scaled = jnp.concatenate(
        [
            x_ref[:, LANES * tile : LANES * (tile + 1)] * pair(to_end, tile, length)
            for tile in range(x_ref.shape[1] // LANES)
        ],
        axis=1,
    )
    state = dot3(b_ref[...], scaled, TN)
    pack(send_ref, state, ranks, pitch)
    heads = ld.shape[0]
    totals = jnp.concatenate([last, jnp.zeros((1, LANES - heads), F32)], axis=1)
    totals = jnp.broadcast_to(totals, (ranks, LANES))
    used = state.size // ranks // LANES
    for spare in range(used, pitch):
        send_ref[pl.ds(spare, ranks, stride=pitch), :] = totals


def local_output(ld_heads, x_ref, b_ref, c_ref, cum_ref, cum_t_ref, skip_ref, y_ref):
    length = x_ref.shape[0]
    row = lax.broadcasted_iota(jnp.int32, (length, length), 0)
    col = lax.broadcasted_iota(jnp.int32, (length, length), 1)
    causal = row >= col
    scores = dot3(c_ref[...], b_ref[...], NT)
    cum = cum_ref[...]
    cum_t = cum_t_ref[...]
    for tile in range(ld_heads // 2):
        parts = []
        for head in (2 * tile, 2 * tile + 1):
            gap = jnp.where(causal, cum_t[:, head : head + 1] - cum[head : head + 1, :], -1e30)
            weights = jnp.exp(gap) * scores
            x = x_ref[:, HEAD * head : HEAD * (head + 1)]
            parts.append(dot3(weights, x, NN) + skip_ref[head] * x)
        y_ref[:, LANES * tile : LANES * (tile + 1)] = jnp.concatenate(parts, axis=1)


def local_grad(ld_heads, dy_ref, b_ref, c_ref, cum_ref, cum_t_ref, skip_ref, dx_ref):
    length = dy_ref.shape[0]
    row = lax.broadcasted_iota(jnp.int32, (length, length), 0)
    col = lax.broadcasted_iota(jnp.int32, (length, length), 1)
    causal = col >= row
    scores = dot3(b_ref[...], c_ref[...], NT)
    cum = cum_ref[...]
    cum_t = cum_t_ref[...]
    for tile in range(ld_heads // 2):
        parts = []
        for head in (2 * tile, 2 * tile + 1):
            gap = jnp.where(causal, cum[head : head + 1, :] - cum_t[:, head : head + 1], -1e30)
            weights = jnp.exp(gap) * scores
            dy = dy_ref[:, HEAD * head : HEAD * (head + 1)]
            parts.append(dot3(weights, dy, NN) + skip_ref[head] * dy)
        dx_ref[:, LANES * tile : LANES * (tile + 1)] = jnp.concatenate(parts, axis=1)


def scan_forward(ranks, pitch, used, width, recv_ref, send_ref, decay_ref):
    tiles = width // LANES
    rows = used // tiles
    totals = recv_ref[pl.ds(used, ranks, stride=pitch), :]
    decays = jnp.exp(totals)
    for tile in range(tiles):
        spread = pair(decays, tile, ranks)
        for r in range(rows):
            decay_ref[pl.ds(tile * rows + r, ranks, stride=pitch), :] = spread
    for spare in range(used, pitch):
        decay_ref[pl.ds(spare, ranks, stride=pitch), :] = decays
    state = jnp.zeros((pitch, LANES), F32)
    for rank in range(ranks):
        here = pl.ds(rank * pitch, pitch)
        send_ref[here, :] = state
        state = state * decay_ref[here, :] + recv_ref[here, :]


def scan_backward(ranks, pitch, recv_ref, decay_ref, send_ref):
    state = jnp.zeros((pitch, LANES), F32)
    for rank in reversed(range(ranks)):
        here = pl.ds(rank * pitch, pitch)
        send_ref[here, :] = state
        state = state * decay_ref[here, :] + recv_ref[here, :]


def gate_out(
    ring, ranks, pitch, io, pos_ref, recv_ref, c_ref, cum_t_ref, y_ref, gate_ref, gain_ref, w_ref,
    gated_ref, normed_ref, scale_ref, far_left_ref, far_right_ref, next_ref, prev_ref, own_ref,
    state_ref, high_ref, low_ref,
):
    length, width = y_ref.shape
    unpack(recv_ref, state_ref, ranks, pitch)
    carried = dot3(c_ref[...], state_ref[...], NN)
    from_start = jnp.exp(cum_t_ref[...])
    total = jnp.zeros((length, LANES), F32)
    for tile in range(width // LANES):
        here = slice(LANES * tile, LANES * (tile + 1))
        y = y_ref[:, here] + carried[:, here] * pair(from_start, tile, length)
        gate = gate_ref[:, here]
        gated = y * (gate / (1.0 + jnp.exp(-gate)))
        gated_ref[:, here] = gated
        total = total + gated * gated
    scale = lax.rsqrt(jnp.sum(total, axis=1, keepdims=True) * (1.0 / width) + EPS)
    scale_ref[...] = jnp.broadcast_to(scale, scale_ref.shape)
    normed_ref[...] = gated_ref[...] * scale * gain_ref[...]
    io.flush(0, 1, 2)
    me = pos_ref[0]
    block = own_ref.shape[0]
    rows = []
    for step in (2, 1, -1, 0):
        index = lax.rem(me + step + ring, ring)
        rows.append(normed_ref[pl.ds(pl.multiple_of(index * block, 8), block), :])
    high_ref[...], low_ref[...] = split(jnp.concatenate(rows, axis=0))
    half = far_left_ref.shape[1]
    for side, far_ref in enumerate((far_left_ref, far_right_ref)):

        @pl.loop(0, half // TILE)
        def _(n):
            k = side * (half // TILE) + n
            io.tile(7, k).wait()
            here = pl.ds(pl.multiple_of(k * TILE, TILE), TILE)
            high, low = split(w_ref[:, here])
            product = dot(high_ref[...], high, NN) + (dot(high_ref[...], low, NN) + dot(low_ref[...], high, NN))
            far_ref[:, pl.ds(pl.multiple_of(n * TILE, TILE), TILE)] = product[:block]
            next_ref[:, here] = product[block : 2 * block]
            prev_ref[:, here] = product[2 * block : 3 * block]
            own_ref[:, here] = product[3 * block :]

        io.flush(3 + side)


def turn(
    ring, rows, pos_ref, own_ref, prev_ref, next_ref, far_left_ref, far_right_ref, normed_ref,
    keep_ref, give_ref, high_ref, low_ref, held_ref, turned_ref,
):
    me, core = pos_ref[0], pos_ref[1]
    block, model = own_ref.shape
    length = normed_ref.shape[0]
    wide, padded = turned_ref.shape
    held_ref[length:, :] = jnp.zeros((padded - length, wide), F32)
    for part in range(model // wide):
        here = slice(part * wide, (part + 1) * wide)
        if part * wide < model // 2:
            far = far_left_ref[:, here]
        else:
            far = far_right_ref[:, part * wide - model // 2 : (part + 1) * wide - model // 2]
        for step, piece in ((0, own_ref[:, here]), (-1, prev_ref[:, here]), (1, next_ref[:, here]), (2, far)):
            index = lax.rem(me + step + ring, ring)
            held_ref[pl.ds(pl.multiple_of(index * block, 8), block), :] = piece
        turned = held_ref[...].T
        turned_ref[...] = turned
        high_ref[here, :], low_ref[here, :] = split(turned)
        for chip in range(wide // (2 * rows)):
            at = (part * wide // (2 * rows) + chip) * rows
            keep_ref[at : at + rows, :] = turned_ref[pl.ds(pl.multiple_of((2 * chip + core) * rows, 8), rows), :]
            give_ref[at : at + rows, :] = turned_ref[pl.ds(pl.multiple_of((2 * chip + 1 - core) * rows, 8), rows), :]
    width = normed_ref.shape[1]
    held_ref[:length, :width] = normed_ref[...]
    give_ref[model // 2 :, :] = held_ref[:, :width].T


def norm_grad(
    ranks, pitch, io, high_ref, low_ref, w_ref, gated_ref, scale_ref, gate_ref, gain_ref, c_ref, cum_t_ref,
    send_ref, dy_ref, sum_ref, dn_ref,
):
    length, width = gated_ref.shape
    sum_ref[...] = jnp.zeros_like(sum_ref)

    @pl.loop(0, w_ref.shape[1] // TILE)
    def _(k):
        io.tile(2, k).wait()
        here = pl.ds(pl.multiple_of(k * TILE, TILE), TILE)
        w_high, w_low = split(w_ref[:, here])
        high, low = high_ref[here, :], low_ref[here, :]
        sum_ref[...] += dot(w_high, high, NN) + (dot(w_high, low, NN) + dot(w_low, high, NN))

    dn_ref[...] = sum_ref[...].T
    scale = scale_ref[:, :1]
    total = jnp.zeros((length, LANES), F32)
    for tile in range(width // LANES):
        here = slice(LANES * tile, LANES * (tile + 1))
        total = total + dn_ref[:length, here] * gain_ref[:, here] * gated_ref[:, here]
    mean = jnp.sum(total, axis=1, keepdims=True) * (1.0 / width)
    shift = scale * scale * scale * mean
    from_start = jnp.exp(cum_t_ref[...])
    scaled = []
    for tile in range(width // LANES):
        here = slice(LANES * tile, LANES * (tile + 1))
        gate = gate_ref[:, here]
        d_gated = dn_ref[:length, here] * gain_ref[:, here] * scale - gated_ref[:, here] * shift
        dy = d_gated * (gate / (1.0 + jnp.exp(-gate)))
        dy_ref[:, here] = dy
        scaled.append(dy * pair(from_start, tile, length))
    grad_state = dot3(c_ref[...], jnp.concatenate(scaled, axis=1), TN)
    pack(send_ref, grad_state, ranks, pitch)
    used = grad_state.size // ranks // LANES
    for spare in range(used, pitch):
        send_ref[pl.ds(spare, ranks, stride=pitch), :] = jnp.zeros((ranks, LANES), F32)


def weight_grad(across, down, io, keep_ref, other_ref, normed_ref, out_ref, n_high_ref, n_low_ref, o_high_ref, o_low_ref):
    length, width = normed_ref.shape
    padded = keep_ref.shape[1]
    rows = keep_ref.shape[0] // (across * down)
    n_high_ref[:length, :], n_low_ref[:length, :] = split(normed_ref[...])
    n_high_ref[length:, :] = jnp.zeros((padded - length, width), BF16)
    n_low_ref[length:, :] = jnp.zeros((padded - length, width), BF16)
    o_high_ref[...], o_low_ref[...] = split(other_ref[keep_ref.shape[0] :, :].T)
    n_high, n_low, o_high, o_low = n_high_ref[...], n_low_ref[...], o_high_ref[...], o_low_ref[...]
    for y in range(down):
        here = slice(y * across * rows, (y + 1) * across * rows)
        k_high, k_low = split(keep_ref[here, :])
        t_high, t_low = split(other_ref[here, :])
        small = dot(k_high, n_low, NN) + dot(k_low, n_high, NN) + dot(t_high, o_low, NN) + dot(t_low, o_high, NN)
        product = dot(k_high, n_high, NN) + dot(t_high, o_high, NN) + small
        for x in range(across):
            at = (x * down + y) * rows
            out_ref[at : at + rows, :] = product[x * rows : (x + 1) * rows]


def sum_column(count, recv_ref, share_ref):
    rows = share_ref.shape[0]
    total = recv_ref[:rows, :]
    for i in range(1, count):
        total = total + recv_ref[i * rows : (i + 1) * rows, :]
    share_ref[...] = total


def pass_on(next_ref, prev_ref, up_ref, down_ref, next_out_ref, prev_out_ref):
    half = up_ref.shape[1]
    next_out_ref[:, :half] = next_ref[:, :half] + up_ref[...]
    next_out_ref[:, half:] = next_ref[:, half:]
    prev_out_ref[:, :half] = prev_ref[:, :half]
    prev_out_ref[:, half:] = prev_ref[:, half:] + down_ref[...]


def finish(ranks, pitch, recv_ref, b_ref, cum_t_ref, part_ref, dx_ref, state_ref):
    length, width = part_ref.shape
    unpack(recv_ref, state_ref, ranks, pitch)
    carried = dot3(b_ref[...], state_ref[...], NN)
    cum_t = cum_t_ref[...]
    to_end = jnp.exp(cum_t[length - 1 :, :] - cum_t)
    for tile in range(width // LANES):
        here = slice(LANES * tile, LANES * (tile + 1))
        dx_ref[:, here] = part_ref[:, here] + carried[:, here] * pair(to_end, tile, length)


def shifted(value, axis, step):
    count = lax.axis_size(axis)
    return lax.ppermute(value, axis, [(i, (i + step) % count) for i in range(count)])


def swapped(value, axis):
    return lax.ppermute(value, axis, [(i, i ^ 1) for i in range(lax.axis_size(axis))])


def exchange(value, axis):
    return lax.all_to_all(value, axis, 0, 0, tiled=True)


def per_device(head_input, gate_input, log_decay, in_b, in_c, skip, norm_gain, w_out, d_out):
    x, gate, ld, b_mat, c_mat, d_own = head_input[0], gate_input[0], log_decay[0], in_b[0], in_c[0], d_out[0]
    length, width = x.shape
    heads, state = ld.shape[0], b_mat.shape[1]
    model = w_out.shape[1]
    ranks, ring, seqs = lax.axis_size("ctx"), lax.axis_size("tp"), lax.axis_size("dp")
    block = d_own.shape[0]
    used = state * width // ranks // LANES
    pitch = -(-(used + 1) // 8) * 8
    pieces = (ranks * pitch, LANES)
    gain = norm_gain[None, :]
    dp = lax.axis_index("dp")
    pos = jnp.stack([lax.axis_index("tp"), lax.rem(lax.axis_index("ctx"), 2), dp]).astype(jnp.int32)
    half = model // 2
    chips = ranks // 2
    rows = model // ranks
    wide = max(width, 2 * rows)
    padded = -(-length // LANES) * LANES
    across = 4 if chips % 16 == 0 else 2
    down = chips // across
    lines = [[y * across + x for x in range(across)] for y in range(down)]
    lines = [
        [[2 * chip + c for chip in line] for line in way for c in range(2)] for way in (lines, list(zip(*lines)))
    ]

    d_prev, d_next = shifted(d_own, "tp", 1), shifted(d_own, "tp", -1)
    far_left, far_right = shifted(d_prev[:, :half], "tp", 1), shifted(d_next[:, half:], "tp", -1)

    send, cum, cum_t = call(
        functools.partial(block_state, ranks, pitch),
        [pieces, (heads, length), (length, heads)],
        [ld, x, b_mat],
        fixed=(0, 1, 2), name="block_state", us=0.3,
    )
    recv = exchange(send, "ctx")
    (y_local,) = call(
        functools.partial(local_output, heads),
        [(length, width)],
        [x, b_mat, c_mat, cum, cum_t, skip],
        smem=(5,), fixed=(0, 1, 2), name="local_output", us=0.3,
    )
    send, decays = call(
        functools.partial(scan_forward, ranks, pitch, used, width),
        [pieces, pieces],
        [recv],
        after=[y_local], name="scan_forward", us=0.3,
    )
    recv = exchange(send, "ctx")
    gated, normed, scale, part_left, part_right, part_next, part_prev, part_own = call(
        functools.partial(gate_out, ring, ranks, pitch),
        [(length, width)] * 2 + [(length, LANES)] + [(block, half)] * 2 + [(block, model)] * 3,
        [pos, recv, c_mat, cum_t, y_local, gate, gain, w_out],
        smem=(0,), tiled=7, fixed=(2, 5, 7), io=True,
        scratch=[pltpu.VMEM((state, width), F32)] + [pltpu.VMEM((length, width), BF16)] * 2,
        name="gate_out", us=7,
    )
    up_far, down_far = shifted(part_left, "tp", 1), shifted(part_right, "tp", -1)
    keep, give, d_high, d_low = call(
        functools.partial(turn, ring, rows),
        [(half, padded), (half + width, padded)] + [jax.ShapeDtypeStruct((model, padded), BF16)] * 2,
        [pos, d_own, d_prev, d_next, far_left, far_right, normed],
        scratch=[pltpu.VMEM((padded, wide), F32), pltpu.VMEM((wide, padded), F32)],
        smem=(0,), name="turn", us=0.3,
    )
    other = swapped(give, "ctx")
    send, dy = call(
        functools.partial(norm_grad, ranks, pitch),
        [pieces, (length, width)],
        [d_high, d_low, w_out, gated, scale, gate, gain, c_mat, cum_t],
        tiled=2, fixed=(2, 5, 7), io=True,
        scratch=[pltpu.VMEM((width, padded), F32), pltpu.VMEM((padded, width), F32)],
        name="norm_grad", us=0.3,
    )
    (grad_w,) = call(
        functools.partial(weight_grad, across, down), [(half, width)], [keep, other, normed],
        scratch=[pltpu.VMEM((padded, width), BF16)] * 4,
        io=True, after=[dy], name="weight_grad", us=0.3,
    )
    grad_w = lax.psum_scatter(grad_w, "ctx", scatter_dimension=0, tiled=True, axis_index_groups=lines[0])
    recv = exchange(send, "ctx")
    (dx_local,) = call(
        functools.partial(local_grad, heads),
        [(length, width)],
        [dy, b_mat, c_mat, cum, cum_t, skip],
        smem=(5,), fixed=(1, 2), name="local_grad", us=0.3,
    )
    part_next, part_prev = call(
        pass_on, [(block, model)] * 2, [part_next, part_prev, up_far, down_far],
        after=[dx_local], name="pass_on", us=0.3,
    )
    up, low = shifted(part_next, "tp", 1), shifted(part_prev, "tp", -1)
    (send,) = call(
        functools.partial(scan_backward, ranks, pitch),
        [pieces],
        [recv, decays],
        after=[part_next], name="scan_backward", us=0.3,
    )
    recv = exchange(send, "ctx")
    (dx,) = call(
        functools.partial(finish, ranks, pitch),
        [(length, width)],
        [recv, b_mat, cum_t, dx_local],
        fixed=(1,),
        scratch=[pltpu.VMEM((state, width), F32)], name="finish", us=0.3,
    )
    out = part_own + up + low
    grad_w, _, out = lax.optimization_barrier((grad_w, dx, out))
    columns = [[seqs * i + p for i in line for p in range(seqs)] for line in lines[1]]
    grad_w = lax.all_to_all(grad_w, ("ctx", "dp"), 0, 0, tiled=True, axis_index_groups=columns)
    (share,) = call(
        functools.partial(sum_column, down * seqs), [(rows // seqs, width)], [grad_w],
        name="sum_column", us=1,
    )
    return (out[None], dx[None], share)


def solution(mesh):
    placed = (
        P("dp", "ctx", "tp"),
        P("dp", "ctx", "tp"),
        P("dp", "tp", "ctx"),
        P("dp", "ctx", None),
        P("dp", "ctx", None),
        P("tp"),
        P("tp"),
        P("tp", None),
        P("dp", ("ctx", "tp"), None),
    )
    return jax.shard_map(
        per_device,
        mesh=mesh,
        in_specs=placed,
        out_specs=(P("dp", ("ctx", "tp"), None), P("dp", "ctx", "tp"), P(("ctx", "dp"), "tp")),
        check_vma=False,
    )
```

```python
import functools
import jax
import jax.numpy as jnp
from jax import lax
from jax.experimental import pallas as pl
from jax.experimental.pallas import tpu as pltpu
from jax.sharding import PartitionSpec as P

F32 = jnp.float32
BF16 = jnp.bfloat16
HEAD = 64
LANES = 128
EPS = 1e-05
NN = ((1,), (0,))
NT = ((1,), (1,))
TN = ((0,), (0,))
HIGHEST = lax.Precision.HIGHEST


def split(a):
    high = a.astype(BF16)
    return high, (a - high.astype(F32)).astype(BF16)


def dot(a, b, dims):
    return lax.dot_general(a, b, (dims, ((), ())), preferred_element_type=F32)


def dot3(a, b, dims):
    a_high, a_low = split(a)
    b_high, b_low = split(b)
    return dot(a_high, b_high, dims) + (dot(a_high, b_low, dims) + dot(a_low, b_high, dims))


TILE = 256


class Copies:
    def __init__(self, sources, held, in_sems, tile_sems, made, targets, out_sems):
        self.sources, self.held, self.in_sems, self.tile_sems = sources, held, in_sems, tile_sems
        self.out = [pltpu.make_async_copy(a, b, out_sems.at[j]) for j, (a, b) in enumerate(zip(made, targets))]
        self.started = set()

    def whole(self, i):
        return pltpu.make_async_copy(self.sources[i], self.held[i], self.in_sems.at[i])

    def tile(self, i, k):
        here = pl.ds(pl.multiple_of(k * TILE, TILE), TILE)
        return pltpu.make_async_copy(self.sources[i].at[:, here], self.held[i].at[:, here], self.tile_sems.at[k])

    def flush(self, *which):
        for j in which:
            self.out[j].start()
            self.started.add(j)


def call(body, outs, ins, name, us, scratch=(), smem=(), tiled=None, after=(), io=False, fixed=(), far=(), vmem=40):
    outs = [o if isinstance(o, jax.ShapeDtypeStruct) else jax.ShapeDtypeStruct(o, F32) for o in outs]
    n, m = len(ins), len(outs)
    big = [i for i in range(n) if i not in smem]
    tiles = ins[tiled].shape[1] // TILE if tiled is not None else 1

    def run(*refs):
        refs = list(refs)
        sources, refs = refs[:n], refs[n + len(after) :]
        targets, refs = refs[:m], refs[m:]
        held, refs = dict(zip(big, refs[: len(big)])), refs[len(big) :]
        made, refs = refs[:m], refs[m:]
        in_sems, tile_sems, out_sems = refs[:3]
        copies = Copies(sources, held, in_sems, tile_sems, made, targets, out_sems)
        for i in big:
            if i != tiled:
                copies.whole(i).start()
        if tiled is not None:
            for k in range(tiles):
                copies.tile(tiled, k).start()
        for i in big:
            if i != tiled:
                copies.whole(i).wait()
        operands = [held.get(i, sources[i]) for i in range(n)]
        body(*([copies] if io else []), *operands, *made, *refs[3:])
        copies.flush(*[j for j in range(m) if j not in copies.started])
        for c in copies.out:
            c.wait()

    return pl.pallas_call(
        run,
        out_shape=[pltpu.HBM(o.shape, o.dtype) if j in far else o for j, o in enumerate(outs)],
        in_specs=[
            *[pl.BlockSpec(memory_space=pltpu.SMEM if i in smem else pltpu.HBM) for i in range(n)],
            *[pl.BlockSpec(memory_space=pltpu.HBM)] * len(after),
        ],
        out_specs=[pl.BlockSpec(memory_space=pltpu.HBM)] * m,
        scratch_shapes=[
            *[pltpu.VMEM(ins[i].shape, ins[i].dtype) for i in big],
            *[pltpu.VMEM(o.shape, o.dtype) for o in outs],
            pltpu.SemaphoreType.DMA((n,)),
            pltpu.SemaphoreType.DMA((tiles,)),
            pltpu.SemaphoreType.DMA((m,)),
            *scratch,
        ],
        compiler_params=pltpu.CompilerParams(vmem_limit_bytes=vmem * 1024 * 1024),
        cost_estimate=pl.CostEstimate(flops=0, bytes_accessed=int(us * 3e6), transcendentals=0),
        name=name,
    )(*[pltpu.with_memory_space_constraint(v, pltpu.HBM) if i in fixed else v for i, v in enumerate(ins)], *after)


def pair(table, tile, rows, turned=False):
    lane = lax.broadcasted_iota(jnp.int32, (rows, LANES), 1)
    return jnp.where(lane < HEAD, table[:, 2 * tile : 2 * tile + 1], table[:, 2 * tile + 1 : 2 * tile + 2])


def pack(send_ref, state, ranks, pitch):
    rows = state.shape[0] // ranks
    for tile in range(state.shape[1] // LANES):
        for r in range(rows):
            send_ref[pl.ds(tile * rows + r, ranks, stride=pitch), :] = state[
                ranks * r : ranks * (r + 1), LANES * tile : LANES * (tile + 1)
            ]


def unpack(recv_ref, state_ref, ranks, pitch):
    rows = state_ref.shape[0] // ranks
    for tile in range(state_ref.shape[1] // LANES):
        for r in range(rows):
            state_ref[ranks * r : ranks * (r + 1), LANES * tile : LANES * (tile + 1)] = recv_ref[
                pl.ds(tile * rows + r, ranks, stride=pitch), :
            ]


def block_state(ranks, pitch, ld_ref, x_ref, b_ref, send_ref, cum_ref, cum_t_ref):
    length = x_ref.shape[0]
    row = lax.broadcasted_iota(jnp.int32, (length, length), 0)
    col = lax.broadcasted_iota(jnp.int32, (length, length), 1)
    upto = jnp.where(row >= col, 1.0, 0.0).astype(F32)
    ld = ld_ref[:, 0, :]
    cum = lax.dot_general(ld, upto, (NT, ((), ())), precision=HIGHEST, preferred_element_type=F32)
    cum_t = lax.dot_general(upto, ld, (NT, ((), ())), precision=HIGHEST, preferred_element_type=F32)
    cum_ref[...] = cum
    cum_t_ref[...] = cum_t
    last = cum_t[length - 1 :, :]
    to_end = jnp.exp(last - cum_t)
    scaled = jnp.concatenate(
        [
            x_ref[:, LANES * tile : LANES * (tile + 1)] * pair(to_end, tile, length)
            for tile in range(x_ref.shape[1] // LANES)
        ],
        axis=1,
    )
    state = dot3(b_ref[...], scaled, TN)
    pack(send_ref, state, ranks, pitch)
    heads = ld.shape[0]
    totals = jnp.concatenate([last, jnp.zeros((1, LANES - heads), F32)], axis=1)
    totals = jnp.broadcast_to(totals, (ranks, LANES))
    used = state.size // ranks // LANES
    for spare in range(used, pitch):
        send_ref[pl.ds(spare, ranks, stride=pitch), :] = totals


def local_output(ld_heads, x_ref, b_ref, c_ref, cum_ref, cum_t_ref, skip_ref, y_ref):
    length = x_ref.shape[0]
    row = lax.broadcasted_iota(jnp.int32, (length, length), 0)
    col = lax.broadcasted_iota(jnp.int32, (length, length), 1)
    causal = row >= col
    scores = dot3(c_ref[...], b_ref[...], NT)
    cum = cum_ref[...]
    cum_t = cum_t_ref[...]
    for tile in range(ld_heads // 2):
        parts = []
        for head in (2 * tile, 2 * tile + 1):
            gap = jnp.where(causal, cum_t[:, head : head + 1] - cum[head : head + 1, :], -1e30)
            weights = jnp.exp(gap) * scores
            x = x_ref[:, HEAD * head : HEAD * (head + 1)]
            parts.append(dot3(weights, x, NN) + skip_ref[head] * x)
        y_ref[:, LANES * tile : LANES * (tile + 1)] = jnp.concatenate(parts, axis=1)


def local_grad(ld_heads, dy_ref, b_ref, c_ref, cum_ref, cum_t_ref, skip_ref, dx_ref):
    length = dy_ref.shape[0]
    row = lax.broadcasted_iota(jnp.int32, (length, length), 0)
    col = lax.broadcasted_iota(jnp.int32, (length, length), 1)
    causal = col >= row
    scores = dot3(b_ref[...], c_ref[...], NT)
    cum = cum_ref[...]
    cum_t = cum_t_ref[...]
    for tile in range(ld_heads // 2):
        parts = []
        for head in (2 * tile, 2 * tile + 1):
            gap = jnp.where(causal, cum[head : head + 1, :] - cum_t[:, head : head + 1], -1e30)
            weights = jnp.exp(gap) * scores
            dy = dy_ref[:, HEAD * head : HEAD * (head + 1)]
            parts.append(dot3(weights, dy, NN) + skip_ref[head] * dy)
        dx_ref[:, LANES * tile : LANES * (tile + 1)] = jnp.concatenate(parts, axis=1)


def scan_forward(ranks, pitch, used, width, recv_ref, send_ref, decay_ref):
    tiles = width // LANES
    rows = used // tiles
    totals = recv_ref[pl.ds(used, ranks, stride=pitch), :]
    decays = jnp.exp(totals)
    for tile in range(tiles):
        spread = pair(decays, tile, ranks)
        for r in range(rows):
            decay_ref[pl.ds(tile * rows + r, ranks, stride=pitch), :] = spread
    for spare in range(used, pitch):
        decay_ref[pl.ds(spare, ranks, stride=pitch), :] = decays
    state = jnp.zeros((pitch, LANES), F32)
    for rank in range(ranks):
        here = pl.ds(rank * pitch, pitch)
        send_ref[here, :] = state
        state = state * decay_ref[here, :] + recv_ref[here, :]


def scan_backward(ranks, pitch, recv_ref, decay_ref, send_ref):
    state = jnp.zeros((pitch, LANES), F32)
    for rank in reversed(range(ranks)):
        here = pl.ds(rank * pitch, pitch)
        send_ref[here, :] = state
        state = state * decay_ref[here, :] + recv_ref[here, :]


def gate_out(
    ring, ranks, pitch, io, pos_ref, recv_ref, c_ref, cum_t_ref, y_ref, gate_ref, gain_ref, w_ref,
    gated_ref, normed_ref, scale_ref, far_left_ref, far_right_ref, next_ref, prev_ref, own_ref,
    state_ref, high_ref, low_ref,
):
    length, width = y_ref.shape
    unpack(recv_ref, state_ref, ranks, pitch)
    carried = dot3(c_ref[...], state_ref[...], NN)
    from_start = jnp.exp(cum_t_ref[...])
    total = jnp.zeros((length, LANES), F32)
    for tile in range(width // LANES):
        here = slice(LANES * tile, LANES * (tile + 1))
        y = y_ref[:, here] + carried[:, here] * pair(from_start, tile, length)
        gate = gate_ref[:, here]
        gated = y * (gate / (1.0 + jnp.exp(-gate)))
        gated_ref[:, here] = gated
        total = total + gated * gated
    scale = lax.rsqrt(jnp.sum(total, axis=1, keepdims=True) * (1.0 / width) + EPS)
    scale_ref[...] = jnp.broadcast_to(scale, scale_ref.shape)
    normed_ref[...] = gated_ref[...] * scale * gain_ref[...]
    io.flush(0, 1, 2)
    me = pos_ref[0]
    block = own_ref.shape[0]
    rows = []
    for step in (2, 1, -1, 0):
        index = lax.rem(me + step + ring, ring)
        rows.append(normed_ref[pl.ds(pl.multiple_of(index * block, 8), block), :])
    high_ref[...], low_ref[...] = split(jnp.concatenate(rows, axis=0))
    half = far_left_ref.shape[1]
    for side, far_ref in enumerate((far_left_ref, far_right_ref)):

        @pl.loop(0, half // TILE)
        def _(n):
            k = side * (half // TILE) + n
            io.tile(7, k).wait()
            here = pl.ds(pl.multiple_of(k * TILE, TILE), TILE)
            high, low = split(w_ref[:, here])
            product = dot(high_ref[...], high, NN) + (dot(high_ref[...], low, NN) + dot(low_ref[...], high, NN))
            far_ref[:, pl.ds(pl.multiple_of(n * TILE, TILE), TILE)] = product[:block]
            next_ref[:, here] = product[block : 2 * block]
            prev_ref[:, here] = product[2 * block : 3 * block]
            own_ref[:, here] = product[3 * block :]

        io.flush(3 + side)


def turn(
    ring, rows, pos_ref, own_ref, prev_ref, next_ref, far_left_ref, far_right_ref, normed_ref,
    keep_ref, give_ref, high_ref, low_ref, held_ref, turned_ref,
):
    me, core = pos_ref[0], pos_ref[1]
    block, model = own_ref.shape
    length = normed_ref.shape[0]
    wide, padded = turned_ref.shape
    held_ref[length:, :] = jnp.zeros((padded - length, wide), F32)
    for part in range(model // wide):
        here = slice(part * wide, (part + 1) * wide)
        if part * wide < model // 2:
            far = far_left_ref[:, here]
        else:
            far = far_right_ref[:, part * wide - model // 2 : (part + 1) * wide - model // 2]
        for step, piece in ((0, own_ref[:, here]), (-1, prev_ref[:, here]), (1, next_ref[:, here]), (2, far)):
            index = lax.rem(me + step + ring, ring)
            held_ref[pl.ds(pl.multiple_of(index * block, 8), block), :] = piece
        turned = held_ref[...].T
        turned_ref[...] = turned
        high_ref[here, :], low_ref[here, :] = split(turned)
        for chip in range(wide // (2 * rows)):
            at = (part * wide // (2 * rows) + chip) * rows
            keep_ref[at : at + rows, :] = turned_ref[pl.ds(pl.multiple_of((2 * chip + core) * rows, 8), rows), :]
            give_ref[at : at + rows, :] = turned_ref[pl.ds(pl.multiple_of((2 * chip + 1 - core) * rows, 8), rows), :]
    width = normed_ref.shape[1]
    held_ref[:length, :width] = normed_ref[...]
    give_ref[model // 2 :, :] = held_ref[:, :width].T


def norm_grad(
    ranks, pitch, io, high_ref, low_ref, w_ref, gated_ref, scale_ref, gate_ref, gain_ref, c_ref, cum_t_ref,
    send_ref, dy_ref, sum_ref, dn_ref,
):
    length, width = gated_ref.shape
    sum_ref[...] = jnp.zeros_like(sum_ref)

    @pl.loop(0, w_ref.shape[1] // TILE)
    def _(k):
        io.tile(2, k).wait()
        here = pl.ds(pl.multiple_of(k * TILE, TILE), TILE)
        w_high, w_low = split(w_ref[:, here])
        high, low = high_ref[here, :], low_ref[here, :]
        sum_ref[...] += dot(w_high, high, NN) + (dot(w_high, low, NN) + dot(w_low, high, NN))

    dn_ref[...] = sum_ref[...].T
    scale = scale_ref[:, :1]
    total = jnp.zeros((length, LANES), F32)
    for tile in range(width // LANES):
        here = slice(LANES * tile, LANES * (tile + 1))
        total = total + dn_ref[:length, here] * gain_ref[:, here] * gated_ref[:, here]
    mean = jnp.sum(total, axis=1, keepdims=True) * (1.0 / width)
    shift = scale * scale * scale * mean
    from_start = jnp.exp(cum_t_ref[...])
    scaled = []
    for tile in range(width // LANES):
        here = slice(LANES * tile, LANES * (tile + 1))
        gate = gate_ref[:, here]
        d_gated = dn_ref[:length, here] * gain_ref[:, here] * scale - gated_ref[:, here] * shift
        dy = d_gated * (gate / (1.0 + jnp.exp(-gate)))
        dy_ref[:, here] = dy
        scaled.append(dy * pair(from_start, tile, length))
    grad_state = dot3(c_ref[...], jnp.concatenate(scaled, axis=1), TN)
    pack(send_ref, grad_state, ranks, pitch)
    used = grad_state.size // ranks // LANES
    for spare in range(used, pitch):
        send_ref[pl.ds(spare, ranks, stride=pitch), :] = jnp.zeros((ranks, LANES), F32)


def weight_grad(across, down, io, keep_ref, other_ref, normed_ref, out_ref, n_high_ref, n_low_ref, o_high_ref, o_low_ref):
    length, width = normed_ref.shape
    padded = keep_ref.shape[1]
    rows = keep_ref.shape[0] // (across * down)
    n_high_ref[:length, :], n_low_ref[:length, :] = split(normed_ref[...])
    n_high_ref[length:, :] = jnp.zeros((padded - length, width), BF16)
    n_low_ref[length:, :] = jnp.zeros((padded - length, width), BF16)
    o_high_ref[...], o_low_ref[...] = split(other_ref[keep_ref.shape[0] :, :].T)
    n_high, n_low, o_high, o_low = n_high_ref[...], n_low_ref[...], o_high_ref[...], o_low_ref[...]
    for y in range(down):
        here = slice(y * across * rows, (y + 1) * across * rows)
        k_high, k_low = split(keep_ref[here, :])
        t_high, t_low = split(other_ref[here, :])
        small = dot(k_high, n_low, NN) + dot(k_low, n_high, NN) + dot(t_high, o_low, NN) + dot(t_low, o_high, NN)
        product = dot(k_high, n_high, NN) + dot(t_high, o_high, NN) + small
        for x in range(across):
            at = (x * down + y) * rows
            out_ref[at : at + rows, :] = product[x * rows : (x + 1) * rows]


def sum_column(count, recv_ref, share_ref):
    rows = share_ref.shape[0]
    total = recv_ref[:rows, :]
    for i in range(1, count):
        total = total + recv_ref[i * rows : (i + 1) * rows, :]
    share_ref[...] = total


def pass_on(next_ref, prev_ref, up_ref, down_ref, next_out_ref, prev_out_ref):
    half = up_ref.shape[1]
    next_out_ref[:, :half] = next_ref[:, :half] + up_ref[...]
    next_out_ref[:, half:] = next_ref[:, half:]
    prev_out_ref[:, :half] = prev_ref[:, :half]
    prev_out_ref[:, half:] = prev_ref[:, half:] + down_ref[...]


def finish(ranks, pitch, recv_ref, b_ref, cum_t_ref, part_ref, dx_ref, state_ref):
    length, width = part_ref.shape
    unpack(recv_ref, state_ref, ranks, pitch)
    carried = dot3(b_ref[...], state_ref[...], NN)
    cum_t = cum_t_ref[...]
    to_end = jnp.exp(cum_t[length - 1 :, :] - cum_t)
    for tile in range(width // LANES):
        here = slice(LANES * tile, LANES * (tile + 1))
        dx_ref[:, here] = part_ref[:, here] + carried[:, here] * pair(to_end, tile, length)


def shifted(value, axis, step):
    count = lax.axis_size(axis)
    return lax.ppermute(value, axis, [(i, (i + step) % count) for i in range(count)])


def swapped(value, axis):
    return lax.ppermute(value, axis, [(i, i ^ 1) for i in range(lax.axis_size(axis))])


def exchange(value, axis):
    return lax.all_to_all(value, axis, 0, 0, tiled=True)


def per_device(head_input, gate_input, log_decay, in_b, in_c, skip, norm_gain, w_out, d_out):
    x, gate, ld, b_mat, c_mat, d_own = head_input[0], gate_input[0], log_decay.transpose(1, 0, 2), in_b[0], in_c[0], d_out[0]
    length, width = x.shape
    heads, state = ld.shape[0], b_mat.shape[1]
    model = w_out.shape[1]
    ranks, ring, seqs = lax.axis_size("ctx"), lax.axis_size("tp"), lax.axis_size("dp")
    block = d_own.shape[0]
    used = state * width // ranks // LANES
    pitch = -(-(used + 1) // 8) * 8
    pieces = (ranks * pitch, LANES)
    gain = norm_gain[None, :]
    dp = lax.axis_index("dp")
    pos = jnp.stack([lax.axis_index("tp"), lax.rem(lax.axis_index("ctx"), 2), dp]).astype(jnp.int32)
    half = model // 2
    chips = ranks // 2
    rows = model // ranks
    wide = max(width, 2 * rows)
    padded = -(-length // LANES) * LANES
    across = 4 if chips % 16 == 0 else 2
    down = chips // across
    lines = [[y * across + x for x in range(across)] for y in range(down)]
    lines = [
        [[2 * chip + c for chip in line] for line in way for c in range(2)] for way in (lines, list(zip(*lines)))
    ]

    d_prev, d_next = shifted(d_own, "tp", 1), shifted(d_own, "tp", -1)
    far_left, far_right = shifted(d_prev[:, :half], "tp", 1), shifted(d_next[:, half:], "tp", -1)

    send, cum, cum_t = call(
        functools.partial(block_state, ranks, pitch),
        [pieces, (heads, length), (length, heads)],
        [ld, x, b_mat],
        fixed=(0, 1, 2), name="block_state", us=0.3,
    )
    recv = exchange(send, "ctx")
    (y_local,) = call(
        functools.partial(local_output, heads),
        [(length, width)],
        [x, b_mat, c_mat, cum, cum_t, skip],
        smem=(5,), fixed=(0, 1, 2), name="local_output", us=0.3,
    )
    send, decays = call(
        functools.partial(scan_forward, ranks, pitch, used, width),
        [pieces, pieces],
        [recv],
        after=[y_local], far=(0, 1), name="scan_forward", us=0.3,
    )
    recv = exchange(send, "ctx")
    gated, normed, scale, part_left, part_right, part_next, part_prev, part_own = call(
        functools.partial(gate_out, ring, ranks, pitch),
        [(length, width)] * 2 + [(length, LANES)] + [(block, half)] * 2 + [(block, model)] * 3,
        [pos, recv, c_mat, cum_t, y_local, gate, gain, w_out],
        smem=(0,), tiled=7, fixed=(2, 5, 7), io=True, far=(3, 4, 5, 6, 7),
        scratch=[pltpu.VMEM((state, width), F32)] + [pltpu.VMEM((length, width), BF16)] * 2,
        name="gate_out", us=7,
    )
    up_far, down_far = shifted(part_left, "tp", 1), shifted(part_right, "tp", -1)
    keep, give, d_high, d_low = call(
        functools.partial(turn, ring, rows),
        [(half, padded), (half + width, padded)] + [jax.ShapeDtypeStruct((model, padded), BF16)] * 2,
        [pos, d_own, d_prev, d_next, far_left, far_right, normed],
        scratch=[pltpu.VMEM((padded, wide), F32), pltpu.VMEM((wide, padded), F32)],
        smem=(0,), name="turn", us=0.3,
    )
    other = swapped(give, "ctx")
    send, dy = call(
        functools.partial(norm_grad, ranks, pitch),
        [pieces, (length, width)],
        [d_high, d_low, w_out, gated, scale, gate, gain, c_mat, cum_t],
        tiled=2, fixed=(2, 5, 7), io=True,
        scratch=[pltpu.VMEM((width, padded), F32), pltpu.VMEM((padded, width), F32)],
        name="norm_grad", us=0.3,
    )
    (grad_w,) = call(
        functools.partial(weight_grad, across, down), [(half, width)], [keep, other, normed],
        scratch=[pltpu.VMEM((padded, width), BF16)] * 4,
        io=True, after=[dy], name="weight_grad", us=0.3,
    )
    grad_w = lax.psum_scatter(grad_w, "ctx", scatter_dimension=0, tiled=True, axis_index_groups=lines[0])
    recv = exchange(send, "ctx")
    (dx_local,) = call(
        functools.partial(local_grad, heads),
        [(length, width)],
        [dy, b_mat, c_mat, cum, cum_t, skip],
        smem=(5,), fixed=(1, 2), name="local_grad", us=0.3,
    )
    part_next, part_prev = call(
        pass_on, [(block, model)] * 2, [part_next, part_prev, up_far, down_far], fixed=(0, 1),
        after=[dx_local], name="pass_on", us=0.3,
    )
    up, low = shifted(part_next, "tp", 1), shifted(part_prev, "tp", -1)
    (send,) = call(
        functools.partial(scan_backward, ranks, pitch),
        [pieces],
        [recv, decays],
        fixed=(1,),
        after=[part_next], name="scan_backward", us=0.3,
    )
    recv = exchange(send, "ctx")
    (dx,) = call(
        functools.partial(finish, ranks, pitch),
        [(length, width)],
        [recv, b_mat, cum_t, dx_local],
        fixed=(1,),
        scratch=[pltpu.VMEM((state, width), F32)], name="finish", us=0.3,
    )
    out = part_own + up + low
    grad_w, *_ = lax.optimization_barrier((grad_w, dx, up, low))
    columns = [[seqs * i + p for i in line for p in range(seqs)] for line in lines[1]]
    grad_w = lax.all_to_all(grad_w, ("ctx", "dp"), 0, 0, tiled=True, axis_index_groups=columns)
    (share,) = call(
        functools.partial(sum_column, down * seqs), [(rows // seqs, width)], [grad_w],
        name="sum_column", us=1,
    )
    return (out[None], dx[None], share)


def solution(mesh):
    placed = (
        P("dp", "ctx", "tp"),
        P("dp", "ctx", "tp"),
        P("dp", "tp", "ctx"),
        P("dp", "ctx", None),
        P("dp", "ctx", None),
        P("tp"),
        P("tp"),
        P("tp", None),
        P("dp", ("ctx", "tp"), None),
    )
    return jax.shard_map(
        per_device,
        mesh=mesh,
        in_specs=placed,
        out_specs=(P("dp", ("ctx", "tp"), None), P("dp", "ctx", "tp"), P(("ctx", "dp"), "tp")),
        check_vma=False,
    )
```

```python
import functools
import jax
import jax.numpy as jnp
from jax import lax
from jax.experimental import pallas as pl
from jax.experimental.pallas import tpu as pltpu
from jax.sharding import PartitionSpec as P

F32 = jnp.float32
BF16 = jnp.bfloat16
HEAD = 64
LANES = 128
EPS = 1e-05
NN = ((1,), (0,))
NT = ((1,), (1,))
TN = ((0,), (0,))
HIGHEST = lax.Precision.HIGHEST


def split(a):
    high = a.astype(BF16)
    return high, (a - high.astype(F32)).astype(BF16)


def dot(a, b, dims):
    return lax.dot_general(a, b, (dims, ((), ())), preferred_element_type=F32)


def dot3(a, b, dims):
    a_high, a_low = split(a)
    b_high, b_low = split(b)
    return dot(a_high, b_high, dims) + (dot(a_high, b_low, dims) + dot(a_low, b_high, dims))


TILE = 256


class Copies:
    def __init__(self, sources, held, in_sems, tile_sems, made, targets, out_sems):
        self.sources, self.held, self.in_sems, self.tile_sems = sources, held, in_sems, tile_sems
        self.out = [pltpu.make_async_copy(a, b, out_sems.at[j]) for j, (a, b) in enumerate(zip(made, targets))]
        self.started = set()

    def whole(self, i):
        return pltpu.make_async_copy(self.sources[i], self.held[i], self.in_sems.at[i])

    def tile(self, i, k):
        here = pl.ds(pl.multiple_of(k * TILE, TILE), TILE)
        return pltpu.make_async_copy(self.sources[i].at[:, here], self.held[i].at[:, here], self.tile_sems.at[k])

    def flush(self, *which):
        for j in which:
            self.out[j].start()
            self.started.add(j)


def call(body, outs, ins, name, us, scratch=(), smem=(), tiled=None, after=(), io=False, fixed=(), far=(), vmem=40):
    outs = [o if isinstance(o, jax.ShapeDtypeStruct) else jax.ShapeDtypeStruct(o, F32) for o in outs]
    n, m = len(ins), len(outs)
    big = [i for i in range(n) if i not in smem]
    tiles = ins[tiled].shape[1] // TILE if tiled is not None else 1

    def run(*refs):
        refs = list(refs)
        sources, refs = refs[:n], refs[n + len(after) :]
        targets, refs = refs[:m], refs[m:]
        held, refs = dict(zip(big, refs[: len(big)])), refs[len(big) :]
        made, refs = refs[:m], refs[m:]
        in_sems, tile_sems, out_sems = refs[:3]
        copies = Copies(sources, held, in_sems, tile_sems, made, targets, out_sems)
        for i in big:
            if i != tiled:
                copies.whole(i).start()
        if tiled is not None:
            for k in range(tiles):
                copies.tile(tiled, k).start()
        for i in big:
            if i != tiled:
                copies.whole(i).wait()
        operands = [held.get(i, sources[i]) for i in range(n)]
        body(*([copies] if io else []), *operands, *made, *refs[3:])
        copies.flush(*[j for j in range(m) if j not in copies.started])
        for c in copies.out:
            c.wait()

    return pl.pallas_call(
        run,
        out_shape=[pltpu.HBM(o.shape, o.dtype) if j in far else o for j, o in enumerate(outs)],
        in_specs=[
            *[pl.BlockSpec(memory_space=pltpu.SMEM if i in smem else pltpu.HBM) for i in range(n)],
            *[pl.BlockSpec(memory_space=pltpu.HBM)] * len(after),
        ],
        out_specs=[pl.BlockSpec(memory_space=pltpu.HBM)] * m,
        scratch_shapes=[
            *[pltpu.VMEM(ins[i].shape, ins[i].dtype) for i in big],
            *[pltpu.VMEM(o.shape, o.dtype) for o in outs],
            pltpu.SemaphoreType.DMA((n,)),
            pltpu.SemaphoreType.DMA((tiles,)),
            pltpu.SemaphoreType.DMA((m,)),
            *scratch,
        ],
        compiler_params=pltpu.CompilerParams(vmem_limit_bytes=vmem * 1024 * 1024),
        cost_estimate=pl.CostEstimate(flops=0, bytes_accessed=int(us * 3e6), transcendentals=0),
        name=name,
    )(*[pltpu.with_memory_space_constraint(v, pltpu.HBM) if i in fixed else v for i, v in enumerate(ins)], *after)


def pair(table, tile, rows, turned=False):
    lane = lax.broadcasted_iota(jnp.int32, (rows, LANES), 1)
    return jnp.where(lane < HEAD, table[:, 2 * tile : 2 * tile + 1], table[:, 2 * tile + 1 : 2 * tile + 2])


def pack(send_ref, state, ranks, pitch):
    rows = state.shape[0] // ranks
    for tile in range(state.shape[1] // LANES):
        for r in range(rows):
            send_ref[pl.ds(tile * rows + r, ranks, stride=pitch), :] = state[
                ranks * r : ranks * (r + 1), LANES * tile : LANES * (tile + 1)
            ]


def unpack(recv_ref, state_ref, ranks, pitch):
    rows = state_ref.shape[0] // ranks
    for tile in range(state_ref.shape[1] // LANES):
        for r in range(rows):
            state_ref[ranks * r : ranks * (r + 1), LANES * tile : LANES * (tile + 1)] = recv_ref[
                pl.ds(tile * rows + r, ranks, stride=pitch), :
            ]


def block_state(ranks, pitch, ld_ref, x_ref, b_ref, send_ref, cum_ref, cum_t_ref):
    length = x_ref.shape[0]
    row = lax.broadcasted_iota(jnp.int32, (length, length), 0)
    col = lax.broadcasted_iota(jnp.int32, (length, length), 1)
    upto = jnp.where(row >= col, 1.0, 0.0).astype(F32)
    ld = ld_ref[:, 0, :]
    cum = lax.dot_general(ld, upto, (NT, ((), ())), precision=HIGHEST, preferred_element_type=F32)
    cum_t = lax.dot_general(upto, ld, (NT, ((), ())), precision=HIGHEST, preferred_element_type=F32)
    cum_ref[...] = cum
    cum_t_ref[...] = cum_t
    last = cum_t[length - 1 :, :]
    to_end = jnp.exp(last - cum_t)
    scaled = jnp.concatenate(
        [
            x_ref[:, LANES * tile : LANES * (tile + 1)] * pair(to_end, tile, length)
            for tile in range(x_ref.shape[1] // LANES)
        ],
        axis=1,
    )
    state = dot3(b_ref[...], scaled, TN)
    pack(send_ref, state, ranks, pitch)
    heads = ld.shape[0]
    totals = jnp.concatenate([last, jnp.zeros((1, LANES - heads), F32)], axis=1)
    totals = jnp.broadcast_to(totals, (ranks, LANES))
    used = state.size // ranks // LANES
    for spare in range(used, pitch):
        send_ref[pl.ds(spare, ranks, stride=pitch), :] = totals


def local_output(ld_heads, x_ref, b_ref, c_ref, cum_ref, cum_t_ref, skip_ref, y_ref):
    length = x_ref.shape[0]
    row = lax.broadcasted_iota(jnp.int32, (length, length), 0)
    col = lax.broadcasted_iota(jnp.int32, (length, length), 1)
    causal = row >= col
    scores = dot3(c_ref[...], b_ref[...], NT)
    cum = cum_ref[...]
    cum_t = cum_t_ref[...]
    for tile in range(ld_heads // 2):
        parts = []
        for head in (2 * tile, 2 * tile + 1):
            gap = jnp.where(causal, cum_t[:, head : head + 1] - cum[head : head + 1, :], -1e30)
            weights = jnp.exp(gap) * scores
            x = x_ref[:, HEAD * head : HEAD * (head + 1)]
            parts.append(dot3(weights, x, NN) + skip_ref[head] * x)
        y_ref[:, LANES * tile : LANES * (tile + 1)] = jnp.concatenate(parts, axis=1)


def local_grad(ld_heads, dy_ref, b_ref, c_ref, cum_ref, cum_t_ref, skip_ref, dx_ref):
    length = dy_ref.shape[0]
    row = lax.broadcasted_iota(jnp.int32, (length, length), 0)
    col = lax.broadcasted_iota(jnp.int32, (length, length), 1)
    causal = col >= row
    scores = dot3(b_ref[...], c_ref[...], NT)
    cum = cum_ref[...]
    cum_t = cum_t_ref[...]
    for tile in range(ld_heads // 2):
        parts = []
        for head in (2 * tile, 2 * tile + 1):
            gap = jnp.where(causal, cum[head : head + 1, :] - cum_t[:, head : head + 1], -1e30)
            weights = jnp.exp(gap) * scores
            dy = dy_ref[:, HEAD * head : HEAD * (head + 1)]
            parts.append(dot3(weights, dy, NN) + skip_ref[head] * dy)
        dx_ref[:, LANES * tile : LANES * (tile + 1)] = jnp.concatenate(parts, axis=1)


def scan_forward(ranks, pitch, used, width, recv_ref, send_ref, decay_ref):
    tiles = width // LANES
    rows = used // tiles
    totals = recv_ref[pl.ds(used, ranks, stride=pitch), :]
    decays = jnp.exp(totals)
    for tile in range(tiles):
        spread = pair(decays, tile, ranks)
        for r in range(rows):
            decay_ref[pl.ds(tile * rows + r, ranks, stride=pitch), :] = spread
    for spare in range(used, pitch):
        decay_ref[pl.ds(spare, ranks, stride=pitch), :] = decays
    state = jnp.zeros((pitch, LANES), F32)
    for rank in range(ranks):
        here = pl.ds(rank * pitch, pitch)
        send_ref[here, :] = state
        state = state * decay_ref[here, :] + recv_ref[here, :]


def scan_backward(ranks, pitch, recv_ref, decay_ref, send_ref):
    state = jnp.zeros((pitch, LANES), F32)
    for rank in reversed(range(ranks)):
        here = pl.ds(rank * pitch, pitch)
        send_ref[here, :] = state
        state = state * decay_ref[here, :] + recv_ref[here, :]


def gate_out(
    ring, ranks, pitch, io, pos_ref, recv_ref, c_ref, cum_t_ref, y_ref, gate_ref, gain_ref, w_ref,
    gated_ref, normed_ref, scale_ref, far_left_ref, far_right_ref, next_ref, prev_ref, own_ref,
    state_ref, high_ref, low_ref,
):
    length, width = y_ref.shape
    unpack(recv_ref, state_ref, ranks, pitch)
    carried = dot3(c_ref[...], state_ref[...], NN)
    from_start = jnp.exp(cum_t_ref[...])
    total = jnp.zeros((length, LANES), F32)
    for tile in range(width // LANES):
        here = slice(LANES * tile, LANES * (tile + 1))
        y = y_ref[:, here] + carried[:, here] * pair(from_start, tile, length)
        gate = gate_ref[:, here]
        gated = y * (gate / (1.0 + jnp.exp(-gate)))
        gated_ref[:, here] = gated
        total = total + gated * gated
    scale = lax.rsqrt(jnp.sum(total, axis=1, keepdims=True) * (1.0 / width) + EPS)
    scale_ref[...] = jnp.broadcast_to(scale, scale_ref.shape)
    normed_ref[...] = gated_ref[...] * scale * gain_ref[...]
    io.flush(0, 1, 2)
    me = pos_ref[0]
    block = own_ref.shape[0]
    rows = []
    for step in (2, 1, -1, 0):
        index = lax.rem(me + step + ring, ring)
        rows.append(normed_ref[pl.ds(pl.multiple_of(index * block, 8), block), :])
    high_ref[...], low_ref[...] = split(jnp.concatenate(rows, axis=0))
    half = far_left_ref.shape[1]
    for side, far_ref in enumerate((far_left_ref, far_right_ref)):

        @pl.loop(0, half // TILE)
        def _(n):
            k = side * (half // TILE) + n
            io.tile(7, k).wait()
            here = pl.ds(pl.multiple_of(k * TILE, TILE), TILE)
            high, low = split(w_ref[:, here])
            product = dot(high_ref[...], high, NN) + (dot(high_ref[...], low, NN) + dot(low_ref[...], high, NN))
            far_ref[:, pl.ds(pl.multiple_of(n * TILE, TILE), TILE)] = product[:block]
            next_ref[:, here] = product[block : 2 * block]
            prev_ref[:, here] = product[2 * block : 3 * block]
            own_ref[:, here] = product[3 * block :]

        io.flush(3 + side)


def turn(
    ring, rows, pos_ref, own_ref, prev_ref, next_ref, far_left_ref, far_right_ref, normed_ref,
    keep_ref, give_ref, high_ref, low_ref, held_ref, turned_ref,
):
    me, core = pos_ref[0], pos_ref[1]
    block, model = own_ref.shape
    length = normed_ref.shape[0]
    wide, padded = turned_ref.shape
    held_ref[length:, :] = jnp.zeros((padded - length, wide), F32)
    for part in range(model // wide):
        here = slice(part * wide, (part + 1) * wide)
        if part * wide < model // 2:
            far = far_left_ref[:, here]
        else:
            far = far_right_ref[:, part * wide - model // 2 : (part + 1) * wide - model // 2]
        for step, piece in ((0, own_ref[:, here]), (-1, prev_ref[:, here]), (1, next_ref[:, here]), (2, far)):
            index = lax.rem(me + step + ring, ring)
            held_ref[pl.ds(pl.multiple_of(index * block, 8), block), :] = piece
        turned = held_ref[...].T
        turned_ref[...] = turned
        high_ref[here, :], low_ref[here, :] = split(turned)
        for chip in range(wide // (2 * rows)):
            at = (part * wide // (2 * rows) + chip) * rows
            keep_ref[at : at + rows, :] = turned_ref[pl.ds(pl.multiple_of((2 * chip + core) * rows, 8), rows), :]
            give_ref[at : at + rows, :] = turned_ref[pl.ds(pl.multiple_of((2 * chip + 1 - core) * rows, 8), rows), :]
    width = normed_ref.shape[1]
    held_ref[:length, :width] = normed_ref[...]
    give_ref[model // 2 :, :] = held_ref[:, :width].T


def normed_grad(io, high_ref, low_ref, w_ref, dn_ref, sum_ref):
    sum_ref[...] = jnp.zeros_like(sum_ref)

    @pl.loop(0, w_ref.shape[1] // TILE)
    def _(k):
        io.tile(2, k).wait()
        here = pl.ds(pl.multiple_of(k * TILE, TILE), TILE)
        w_high, w_low = split(w_ref[:, here])
        high, low = high_ref[here, :], low_ref[here, :]
        sum_ref[...] += dot(w_high, high, NN) + (dot(w_high, low, NN) + dot(w_low, high, NN))

    dn_ref[...] = sum_ref[...].T[: dn_ref.shape[0]]


def norm_grad(
    ranks, pitch, dn_ref, gated_ref, scale_ref, gate_ref, gain_ref, c_ref, cum_t_ref, send_ref, dy_ref
):
    length, width = gated_ref.shape
    scale = scale_ref[:, :1]
    total = jnp.zeros((length, LANES), F32)
    for tile in range(width // LANES):
        here = slice(LANES * tile, LANES * (tile + 1))
        total = total + dn_ref[:, here] * gain_ref[:, here] * gated_ref[:, here]
    mean = jnp.sum(total, axis=1, keepdims=True) * (1.0 / width)
    shift = scale * scale * scale * mean
    from_start = jnp.exp(cum_t_ref[...])
    scaled = []
    for tile in range(width // LANES):
        here = slice(LANES * tile, LANES * (tile + 1))
        gate = gate_ref[:, here]
        d_gated = dn_ref[:, here] * gain_ref[:, here] * scale - gated_ref[:, here] * shift
        dy = d_gated * (gate / (1.0 + jnp.exp(-gate)))
        dy_ref[:, here] = dy
        scaled.append(dy * pair(from_start, tile, length))
    grad_state = dot3(c_ref[...], jnp.concatenate(scaled, axis=1), TN)
    pack(send_ref, grad_state, ranks, pitch)
    used = grad_state.size // ranks // LANES
    for spare in range(used, pitch):
        send_ref[pl.ds(spare, ranks, stride=pitch), :] = jnp.zeros((ranks, LANES), F32)


def weight_grad(across, down, io, keep_ref, other_ref, normed_ref, out_ref, n_high_ref, n_low_ref, o_high_ref, o_low_ref):
    length, width = normed_ref.shape
    padded = keep_ref.shape[1]
    rows = keep_ref.shape[0] // (across * down)
    n_high_ref[:length, :], n_low_ref[:length, :] = split(normed_ref[...])
    n_high_ref[length:, :] = jnp.zeros((padded - length, width), BF16)
    n_low_ref[length:, :] = jnp.zeros((padded - length, width), BF16)
    o_high_ref[...], o_low_ref[...] = split(other_ref[keep_ref.shape[0] :, :].T)
    n_high, n_low, o_high, o_low = n_high_ref[...], n_low_ref[...], o_high_ref[...], o_low_ref[...]
    for y in range(down):
        here = slice(y * across * rows, (y + 1) * across * rows)
        k_high, k_low = split(keep_ref[here, :])
        t_high, t_low = split(other_ref[here, :])
        small = dot(k_high, n_low, NN) + dot(k_low, n_high, NN) + dot(t_high, o_low, NN) + dot(t_low, o_high, NN)
        product = dot(k_high, n_high, NN) + dot(t_high, o_high, NN) + small
        for x in range(across):
            at = (x * down + y) * rows
            out_ref[at : at + rows, :] = product[x * rows : (x + 1) * rows]


def sum_column(count, recv_ref, share_ref):
    rows = share_ref.shape[0]
    total = recv_ref[:rows, :]
    for i in range(1, count):
        total = total + recv_ref[i * rows : (i + 1) * rows, :]
    share_ref[...] = total


def pass_on(next_ref, prev_ref, up_ref, down_ref, next_out_ref, prev_out_ref):
    half = up_ref.shape[1]
    next_out_ref[:, :half] = next_ref[:, :half] + up_ref[...]
    next_out_ref[:, half:] = next_ref[:, half:]
    prev_out_ref[:, :half] = prev_ref[:, :half]
    prev_out_ref[:, half:] = prev_ref[:, half:] + down_ref[...]


def finish(ranks, pitch, recv_ref, b_ref, cum_t_ref, part_ref, dx_ref, state_ref):
    length, width = part_ref.shape
    unpack(recv_ref, state_ref, ranks, pitch)
    carried = dot3(b_ref[...], state_ref[...], NN)
    cum_t = cum_t_ref[...]
    to_end = jnp.exp(cum_t[length - 1 :, :] - cum_t)
    for tile in range(width // LANES):
        here = slice(LANES * tile, LANES * (tile + 1))
        dx_ref[:, here] = part_ref[:, here] + carried[:, here] * pair(to_end, tile, length)


def shifted(value, axis, step):
    count = lax.axis_size(axis)
    return lax.ppermute(value, axis, [(i, (i + step) % count) for i in range(count)])


def swapped(value, axis):
    return lax.ppermute(value, axis, [(i, i ^ 1) for i in range(lax.axis_size(axis))])


def exchange(value, axis):
    return lax.all_to_all(value, axis, 0, 0, tiled=True)


def per_device(head_input, gate_input, log_decay, in_b, in_c, skip, norm_gain, w_out, d_out):
    x, gate, ld, b_mat, c_mat, d_own = head_input[0], gate_input[0], log_decay.transpose(1, 0, 2), in_b[0], in_c[0], d_out[0]
    length, width = x.shape
    heads, state = ld.shape[0], b_mat.shape[1]
    model = w_out.shape[1]
    ranks, ring, seqs = lax.axis_size("ctx"), lax.axis_size("tp"), lax.axis_size("dp")
    block = d_own.shape[0]
    used = state * width // ranks // LANES
    pitch = -(-(used + 1) // 8) * 8
    pieces = (ranks * pitch, LANES)
    gain = norm_gain[None, :]
    dp = lax.axis_index("dp")
    pos = jnp.stack([lax.axis_index("tp"), lax.rem(lax.axis_index("ctx"), 2), dp]).astype(jnp.int32)
    half = model // 2
    chips = ranks // 2
    rows = model // ranks
    wide = max(width, 2 * rows)
    padded = -(-length // LANES) * LANES
    across = 4 if chips % 16 == 0 else 2
    down = chips // across
    lines = [[y * across + x for x in range(across)] for y in range(down)]
    lines = [
        [[2 * chip + c for chip in line] for line in way for c in range(2)] for way in (lines, list(zip(*lines)))
    ]

    d_prev, d_next = shifted(d_own, "tp", 1), shifted(d_own, "tp", -1)
    far_left, far_right = shifted(d_prev[:, :half], "tp", 1), shifted(d_next[:, half:], "tp", -1)

    send, cum, cum_t = call(
        functools.partial(block_state, ranks, pitch),
        [pieces, (heads, length), (length, heads)],
        [ld, x, b_mat],
        fixed=(0, 1, 2), name="block_state", us=0.3,
    )
    recv = exchange(send, "ctx")
    (y_local,) = call(
        functools.partial(local_output, heads),
        [(length, width)],
        [x, b_mat, c_mat, cum, cum_t, skip],
        smem=(5,), fixed=(0, 1, 2), name="local_output", us=0.3,
    )
    send, decays = call(
        functools.partial(scan_forward, ranks, pitch, used, width),
        [pieces, pieces],
        [recv],
        after=[y_local], far=(0, 1), name="scan_forward", us=0.3,
    )
    recv = exchange(send, "ctx")
    gated, normed, scale, part_left, part_right, part_next, part_prev, part_own = call(
        functools.partial(gate_out, ring, ranks, pitch),
        [(length, width)] * 2 + [(length, LANES)] + [(block, half)] * 2 + [(block, model)] * 3,
        [pos, recv, c_mat, cum_t, y_local, gate, gain, w_out],
        smem=(0,), tiled=7, fixed=(2, 5, 7), io=True, far=(3, 4, 5, 6, 7),
        scratch=[pltpu.VMEM((state, width), F32)] + [pltpu.VMEM((length, width), BF16)] * 2,
        name="gate_out", us=7,
    )
    up_far, down_far = shifted(part_left, "tp", 1), shifted(part_right, "tp", -1)
    keep, give, d_high, d_low = call(
        functools.partial(turn, ring, rows),
        [(half, padded), (half + width, padded)] + [jax.ShapeDtypeStruct((model, padded), BF16)] * 2,
        [pos, d_own, d_prev, d_next, far_left, far_right, normed],
        scratch=[pltpu.VMEM((padded, wide), F32), pltpu.VMEM((wide, padded), F32)],
        smem=(0,), name="turn", us=0.3,
    )
    other = swapped(give, "ctx")
    (d_normed,) = call(
        normed_grad, [(length, width)], [d_high, d_low, w_out],
        tiled=2, fixed=(2,), io=True, scratch=[pltpu.VMEM((width, padded), F32)], name="normed_grad", us=0.3,
    )
    (grad_w,) = call(
        functools.partial(weight_grad, across, down), [(half, width)], [keep, other, normed],
        scratch=[pltpu.VMEM((padded, width), BF16)] * 4,
        io=True, after=[d_normed], name="weight_grad", us=0.3,
    )
    whole = grad_w
    grad_w = lax.psum_scatter(grad_w, "ctx", scatter_dimension=0, tiled=True, axis_index_groups=lines[0])
    send, dy = call(
        functools.partial(norm_grad, ranks, pitch),
        [pieces, (length, width)],
        [d_normed, gated, scale, gate, gain, c_mat, cum_t],
        fixed=(3,), after=[whole], name="norm_grad", us=0.3,
    )
    recv = exchange(send, "ctx")
    (dx_local,) = call(
        functools.partial(local_grad, heads),
        [(length, width)],
        [dy, b_mat, c_mat, cum, cum_t, skip],
        smem=(5,), fixed=(1, 2), name="local_grad", us=0.3,
    )
    part_next, part_prev = call(
        pass_on, [(block, model)] * 2, [part_next, part_prev, up_far, down_far], fixed=(0, 1),
        after=[dx_local], name="pass_on", us=0.3,
    )
    up, low = shifted(part_next, "tp", 1), shifted(part_prev, "tp", -1)
    (send,) = call(
        functools.partial(scan_backward, ranks, pitch),
        [pieces],
        [recv, decays],
        fixed=(1,),
        after=[part_next], name="scan_backward", us=0.3,
    )
    recv = exchange(send, "ctx")
    (dx,) = call(
        functools.partial(finish, ranks, pitch),
        [(length, width)],
        [recv, b_mat, cum_t, dx_local],
        fixed=(1,),
        scratch=[pltpu.VMEM((state, width), F32)], name="finish", us=0.3,
    )
    out = part_own + up + low
    grad_w, *_ = lax.optimization_barrier((grad_w, dx, up, low))
    columns = [[seqs * i + p for i in line for p in range(seqs)] for line in lines[1]]
    grad_w = lax.all_to_all(grad_w, ("ctx", "dp"), 0, 0, tiled=True, axis_index_groups=columns)
    (share,) = call(
        functools.partial(sum_column, down * seqs), [(rows // seqs, width)], [grad_w],
        name="sum_column", us=1,
    )
    return (out[None], dx[None], share)


def solution(mesh):
    placed = (
        P("dp", "ctx", "tp"),
        P("dp", "ctx", "tp"),
        P("dp", "tp", "ctx"),
        P("dp", "ctx", None),
        P("dp", "ctx", None),
        P("tp"),
        P("tp"),
        P("tp", None),
        P("dp", ("ctx", "tp"), None),
    )
    return jax.shard_map(
        per_device,
        mesh=mesh,
        in_specs=placed,
        out_specs=(P("dp", ("ctx", "tp"), None), P("dp", "ctx", "tp"), P(("ctx", "dp"), "tp")),
        check_vma=False,
    )
```

```python
import functools
import jax
import jax.numpy as jnp
from jax import lax
from jax.experimental import pallas as pl
from jax.experimental.pallas import tpu as pltpu
from jax.sharding import PartitionSpec as P

F32 = jnp.float32
BF16 = jnp.bfloat16
HEAD = 64
LANES = 128
EPS = 1e-05
NN = ((1,), (0,))
NT = ((1,), (1,))
TN = ((0,), (0,))
HIGHEST = lax.Precision.HIGHEST


def split(a):
    high = a.astype(BF16)
    return high, (a - high.astype(F32)).astype(BF16)


def dot(a, b, dims):
    return lax.dot_general(a, b, (dims, ((), ())), preferred_element_type=F32)


def dot3(a, b, dims):
    a_high, a_low = split(a)
    b_high, b_low = split(b)
    return dot(a_high, b_high, dims) + (dot(a_high, b_low, dims) + dot(a_low, b_high, dims))


TILE = 256


class Copies:
    def __init__(self, sources, held, in_sems, tile_sems, made, targets, out_sems):
        self.sources, self.held, self.in_sems, self.tile_sems = sources, held, in_sems, tile_sems
        self.out = [pltpu.make_async_copy(a, b, out_sems.at[j]) for j, (a, b) in enumerate(zip(made, targets))]
        self.started = set()

    def whole(self, i):
        return pltpu.make_async_copy(self.sources[i], self.held[i], self.in_sems.at[i])

    def tile(self, i, k):
        here = pl.ds(pl.multiple_of(k * TILE, TILE), TILE)
        return pltpu.make_async_copy(self.sources[i].at[:, here], self.held[i].at[:, here], self.tile_sems.at[k])

    def flush(self, *which):
        for j in which:
            self.out[j].start()
            self.started.add(j)


def call(body, outs, ins, name, us, scratch=(), smem=(), tiled=None, after=(), io=False, fixed=(), far=(), vmem=40):
    outs = [o if isinstance(o, jax.ShapeDtypeStruct) else jax.ShapeDtypeStruct(o, F32) for o in outs]
    n, m = len(ins), len(outs)
    big = [i for i in range(n) if i not in smem]
    tiles = ins[tiled].shape[1] // TILE if tiled is not None else 1

    def run(*refs):
        refs = list(refs)
        sources, refs = refs[:n], refs[n + len(after) :]
        targets, refs = refs[:m], refs[m:]
        held, refs = dict(zip(big, refs[: len(big)])), refs[len(big) :]
        made, refs = refs[:m], refs[m:]
        in_sems, tile_sems, out_sems = refs[:3]
        copies = Copies(sources, held, in_sems, tile_sems, made, targets, out_sems)
        for i in big:
            if i != tiled:
                copies.whole(i).start()
        if tiled is not None:
            for k in range(tiles):
                copies.tile(tiled, k).start()
        for i in big:
            if i != tiled:
                copies.whole(i).wait()
        operands = [held.get(i, sources[i]) for i in range(n)]
        body(*([copies] if io else []), *operands, *made, *refs[3:])
        copies.flush(*[j for j in range(m) if j not in copies.started])
        for c in copies.out:
            c.wait()

    return pl.pallas_call(
        run,
        out_shape=[pltpu.HBM(o.shape, o.dtype) if j in far else o for j, o in enumerate(outs)],
        in_specs=[
            *[pl.BlockSpec(memory_space=pltpu.SMEM if i in smem else pltpu.HBM) for i in range(n)],
            *[pl.BlockSpec(memory_space=pltpu.HBM)] * len(after),
        ],
        out_specs=[pl.BlockSpec(memory_space=pltpu.HBM)] * m,
        scratch_shapes=[
            *[pltpu.VMEM(ins[i].shape, ins[i].dtype) for i in big],
            *[pltpu.VMEM(o.shape, o.dtype) for o in outs],
            pltpu.SemaphoreType.DMA((n,)),
            pltpu.SemaphoreType.DMA((tiles,)),
            pltpu.SemaphoreType.DMA((m,)),
            *scratch,
        ],
        compiler_params=pltpu.CompilerParams(vmem_limit_bytes=vmem * 1024 * 1024),
        cost_estimate=pl.CostEstimate(flops=0, bytes_accessed=int(us * 3e6), transcendentals=0),
        name=name,
    )(*[pltpu.with_memory_space_constraint(v, pltpu.HBM) if i in fixed else v for i, v in enumerate(ins)], *after)


def pair(table, tile, rows, turned=False):
    lane = lax.broadcasted_iota(jnp.int32, (rows, LANES), 1)
    return jnp.where(lane < HEAD, table[:, 2 * tile : 2 * tile + 1], table[:, 2 * tile + 1 : 2 * tile + 2])


def pack(send_ref, state, ranks, pitch):
    rows = state.shape[0] // ranks
    for tile in range(state.shape[1] // LANES):
        for r in range(rows):
            send_ref[pl.ds(tile * rows + r, ranks, stride=pitch), :] = state[
                ranks * r : ranks * (r + 1), LANES * tile : LANES * (tile + 1)
            ]


def unpack(recv_ref, state_ref, ranks, pitch):
    rows = state_ref.shape[0] // ranks
    for tile in range(state_ref.shape[1] // LANES):
        for r in range(rows):
            state_ref[ranks * r : ranks * (r + 1), LANES * tile : LANES * (tile + 1)] = recv_ref[
                pl.ds(tile * rows + r, ranks, stride=pitch), :
            ]


def block_state(ranks, pitch, ld_ref, x_ref, b_ref, send_ref, cum_ref, cum_t_ref):
    length = x_ref.shape[0]
    row = lax.broadcasted_iota(jnp.int32, (length, length), 0)
    col = lax.broadcasted_iota(jnp.int32, (length, length), 1)
    upto = jnp.where(row >= col, 1.0, 0.0).astype(F32)
    ld = ld_ref[:, 0, :]
    cum = lax.dot_general(ld, upto, (NT, ((), ())), precision=HIGHEST, preferred_element_type=F32)
    cum_t = lax.dot_general(upto, ld, (NT, ((), ())), precision=HIGHEST, preferred_element_type=F32)
    cum_ref[...] = cum
    cum_t_ref[...] = cum_t
    last = cum_t[length - 1 :, :]
    to_end = jnp.exp(last - cum_t)
    scaled = jnp.concatenate(
        [
            x_ref[:, LANES * tile : LANES * (tile + 1)] * pair(to_end, tile, length)
            for tile in range(x_ref.shape[1] // LANES)
        ],
        axis=1,
    )
    state = dot3(b_ref[...], scaled, TN)
    pack(send_ref, state, ranks, pitch)
    heads = ld.shape[0]
    totals = jnp.concatenate([last, jnp.zeros((1, LANES - heads), F32)], axis=1)
    totals = jnp.broadcast_to(totals, (ranks, LANES))
    used = state.size // ranks // LANES
    for spare in range(used, pitch):
        send_ref[pl.ds(spare, ranks, stride=pitch), :] = totals


def local_output(ld_heads, x_ref, b_ref, c_ref, cum_ref, cum_t_ref, skip_ref, y_ref):
    length = x_ref.shape[0]
    row = lax.broadcasted_iota(jnp.int32, (length, length), 0)
    col = lax.broadcasted_iota(jnp.int32, (length, length), 1)
    causal = row >= col
    scores = dot3(c_ref[...], b_ref[...], NT)
    cum = cum_ref[...]
    cum_t = cum_t_ref[...]
    for tile in range(ld_heads // 2):
        parts = []
        for head in (2 * tile, 2 * tile + 1):
            gap = jnp.where(causal, cum_t[:, head : head + 1] - cum[head : head + 1, :], -1e30)
            weights = jnp.exp(gap) * scores
            x = x_ref[:, HEAD * head : HEAD * (head + 1)]
            parts.append(dot3(weights, x, NN) + skip_ref[head] * x)
        y_ref[:, LANES * tile : LANES * (tile + 1)] = jnp.concatenate(parts, axis=1)


def local_grad(ld_heads, dy_ref, b_ref, c_ref, cum_ref, cum_t_ref, skip_ref, dx_ref):
    length = dy_ref.shape[0]
    row = lax.broadcasted_iota(jnp.int32, (length, length), 0)
    col = lax.broadcasted_iota(jnp.int32, (length, length), 1)
    causal = col >= row
    scores = dot3(b_ref[...], c_ref[...], NT)
    cum = cum_ref[...]
    cum_t = cum_t_ref[...]
    for tile in range(ld_heads // 2):
        parts = []
        for head in (2 * tile, 2 * tile + 1):
            gap = jnp.where(causal, cum[head : head + 1, :] - cum_t[:, head : head + 1], -1e30)
            weights = jnp.exp(gap) * scores
            dy = dy_ref[:, HEAD * head : HEAD * (head + 1)]
            parts.append(dot3(weights, dy, NN) + skip_ref[head] * dy)
        dx_ref[:, LANES * tile : LANES * (tile + 1)] = jnp.concatenate(parts, axis=1)


def scan_forward(ranks, pitch, used, width, recv_ref, send_ref, decay_ref):
    tiles = width // LANES
    rows = used // tiles
    totals = recv_ref[pl.ds(used, ranks, stride=pitch), :]
    decays = jnp.exp(totals)
    for tile in range(tiles):
        spread = pair(decays, tile, ranks)
        for r in range(rows):
            decay_ref[pl.ds(tile * rows + r, ranks, stride=pitch), :] = spread
    for spare in range(used, pitch):
        decay_ref[pl.ds(spare, ranks, stride=pitch), :] = decays
    state = jnp.zeros((pitch, LANES), F32)
    for rank in range(ranks):
        here = pl.ds(rank * pitch, pitch)
        send_ref[here, :] = state
        state = state * decay_ref[here, :] + recv_ref[here, :]


def scan_backward(ranks, pitch, recv_ref, decay_ref, send_ref):
    state = jnp.zeros((pitch, LANES), F32)
    for rank in reversed(range(ranks)):
        here = pl.ds(rank * pitch, pitch)
        send_ref[here, :] = state
        state = state * decay_ref[here, :] + recv_ref[here, :]


def gate_out(
    ring, ranks, pitch, io, pos_ref, recv_ref, c_ref, cum_t_ref, y_ref, gate_ref, gain_ref, w_ref,
    gated_ref, normed_ref, scale_ref, far_left_ref, far_right_ref, next_ref, prev_ref, own_ref,
    state_ref, high_ref, low_ref,
):
    length, width = y_ref.shape
    unpack(recv_ref, state_ref, ranks, pitch)
    carried = dot3(c_ref[...], state_ref[...], NN)
    from_start = jnp.exp(cum_t_ref[...])
    total = jnp.zeros((length, LANES), F32)
    for tile in range(width // LANES):
        here = slice(LANES * tile, LANES * (tile + 1))
        y = y_ref[:, here] + carried[:, here] * pair(from_start, tile, length)
        gate = gate_ref[:, here]
        gated = y * (gate / (1.0 + jnp.exp(-gate)))
        gated_ref[:, here] = gated
        total = total + gated * gated
    scale = lax.rsqrt(jnp.sum(total, axis=1, keepdims=True) * (1.0 / width) + EPS)
    scale_ref[...] = jnp.broadcast_to(scale, scale_ref.shape)
    normed_ref[...] = gated_ref[...] * scale * gain_ref[...]
    io.flush(0, 1, 2)
    me = pos_ref[0]
    block = own_ref.shape[0]
    rows = []
    for step in (2, 1, -1, 0):
        index = lax.rem(me + step + ring, ring)
        rows.append(normed_ref[pl.ds(pl.multiple_of(index * block, 8), block), :])
    high_ref[...], low_ref[...] = split(jnp.concatenate(rows, axis=0))
    half = far_left_ref.shape[1]
    for side, far_ref in enumerate((far_left_ref, far_right_ref)):

        @pl.loop(0, half // TILE, unroll=5)
        def _(n):
            k = side * (half // TILE) + n
            io.tile(7, k).wait()
            here = pl.ds(pl.multiple_of(k * TILE, TILE), TILE)
            high, low = split(w_ref[:, here])
            product = dot(high_ref[...], high, NN) + (dot(high_ref[...], low, NN) + dot(low_ref[...], high, NN))
            far_ref[:, pl.ds(pl.multiple_of(n * TILE, TILE), TILE)] = product[:block]
            next_ref[:, here] = product[block : 2 * block]
            prev_ref[:, here] = product[2 * block : 3 * block]
            own_ref[:, here] = product[3 * block :]

        io.flush(3 + side)


def turn(
    ring, rows, pos_ref, own_ref, prev_ref, next_ref, far_left_ref, far_right_ref, normed_ref,
    keep_ref, give_ref, high_ref, low_ref, held_ref, turned_ref,
):
    me, core = pos_ref[0], pos_ref[1]
    block, model = own_ref.shape
    length = normed_ref.shape[0]
    wide, padded = turned_ref.shape
    held_ref[length:, :] = jnp.zeros((padded - length, wide), F32)
    for part in range(model // wide):
        here = slice(part * wide, (part + 1) * wide)
        if part * wide < model // 2:
            far = far_left_ref[:, here]
        else:
            far = far_right_ref[:, part * wide - model // 2 : (part + 1) * wide - model // 2]
        for step, piece in ((0, own_ref[:, here]), (-1, prev_ref[:, here]), (1, next_ref[:, here]), (2, far)):
            index = lax.rem(me + step + ring, ring)
            held_ref[pl.ds(pl.multiple_of(index * block, 8), block), :] = piece
        turned = held_ref[...].T
        turned_ref[...] = turned
        high_ref[here, :], low_ref[here, :] = split(turned)
        for chip in range(wide // (2 * rows)):
            at = (part * wide // (2 * rows) + chip) * rows
            keep_ref[at : at + rows, :] = turned_ref[pl.ds(pl.multiple_of((2 * chip + core) * rows, 8), rows), :]
            give_ref[at : at + rows, :] = turned_ref[pl.ds(pl.multiple_of((2 * chip + 1 - core) * rows, 8), rows), :]
    width = normed_ref.shape[1]
    held_ref[:length, :width] = normed_ref[...]
    give_ref[model // 2 :, :] = held_ref[:, :width].T


def normed_grad(io, high_ref, low_ref, w_ref, dn_ref, sum_ref):
    sum_ref[...] = jnp.zeros_like(sum_ref)

    @pl.loop(0, w_ref.shape[1] // TILE, unroll=5)
    def _(k):
        io.tile(2, k).wait()
        here = pl.ds(pl.multiple_of(k * TILE, TILE), TILE)
        w_high, w_low = split(w_ref[:, here])
        high, low = high_ref[here, :], low_ref[here, :]
        sum_ref[...] += dot(w_high, high, NN) + (dot(w_high, low, NN) + dot(w_low, high, NN))

    dn_ref[...] = sum_ref[...].T[: dn_ref.shape[0]]


def norm_grad(
    ranks, pitch, dn_ref, gated_ref, scale_ref, gate_ref, gain_ref, c_ref, cum_t_ref, send_ref, dy_ref
):
    length, width = gated_ref.shape
    scale = scale_ref[:, :1]
    total = jnp.zeros((length, LANES), F32)
    for tile in range(width // LANES):
        here = slice(LANES * tile, LANES * (tile + 1))
        total = total + dn_ref[:, here] * gain_ref[:, here] * gated_ref[:, here]
    mean = jnp.sum(total, axis=1, keepdims=True) * (1.0 / width)
    shift = scale * scale * scale * mean
    from_start = jnp.exp(cum_t_ref[...])
    scaled = []
    for tile in range(width // LANES):
        here = slice(LANES * tile, LANES * (tile + 1))
        gate = gate_ref[:, here]
        d_gated = dn_ref[:, here] * gain_ref[:, here] * scale - gated_ref[:, here] * shift
        dy = d_gated * (gate / (1.0 + jnp.exp(-gate)))
        dy_ref[:, here] = dy
        scaled.append(dy * pair(from_start, tile, length))
    grad_state = dot3(c_ref[...], jnp.concatenate(scaled, axis=1), TN)
    pack(send_ref, grad_state, ranks, pitch)
    used = grad_state.size // ranks // LANES
    for spare in range(used, pitch):
        send_ref[pl.ds(spare, ranks, stride=pitch), :] = jnp.zeros((ranks, LANES), F32)


def weight_grad(across, down, io, keep_ref, other_ref, normed_ref, out_ref, n_high_ref, n_low_ref, o_high_ref, o_low_ref):
    length, width = normed_ref.shape
    padded = keep_ref.shape[1]
    rows = keep_ref.shape[0] // (across * down)
    n_high_ref[:length, :], n_low_ref[:length, :] = split(normed_ref[...])
    n_high_ref[length:, :] = jnp.zeros((padded - length, width), BF16)
    n_low_ref[length:, :] = jnp.zeros((padded - length, width), BF16)
    o_high_ref[...], o_low_ref[...] = split(other_ref[keep_ref.shape[0] :, :].T)
    n_high, n_low, o_high, o_low = n_high_ref[...], n_low_ref[...], o_high_ref[...], o_low_ref[...]
    for y in range(down):
        here = slice(y * across * rows, (y + 1) * across * rows)
        k_high, k_low = split(keep_ref[here, :])
        t_high, t_low = split(other_ref[here, :])
        small = dot(k_high, n_low, NN) + dot(k_low, n_high, NN) + dot(t_high, o_low, NN) + dot(t_low, o_high, NN)
        product = dot(k_high, n_high, NN) + dot(t_high, o_high, NN) + small
        for x in range(across):
            at = (x * down + y) * rows
            out_ref[at : at + rows, :] = product[x * rows : (x + 1) * rows]


def sum_column(count, recv_ref, share_ref):
    rows = share_ref.shape[0]
    total = recv_ref[:rows, :]
    for i in range(1, count):
        total = total + recv_ref[i * rows : (i + 1) * rows, :]
    share_ref[...] = total


def pass_on(next_ref, prev_ref, up_ref, down_ref, next_out_ref, prev_out_ref):
    half = up_ref.shape[1]
    next_out_ref[:, :half] = next_ref[:, :half] + up_ref[...]
    next_out_ref[:, half:] = next_ref[:, half:]
    prev_out_ref[:, :half] = prev_ref[:, :half]
    prev_out_ref[:, half:] = prev_ref[:, half:] + down_ref[...]


def finish(ranks, pitch, recv_ref, b_ref, cum_t_ref, part_ref, dx_ref, state_ref):
    length, width = part_ref.shape
    unpack(recv_ref, state_ref, ranks, pitch)
    carried = dot3(b_ref[...], state_ref[...], NN)
    cum_t = cum_t_ref[...]
    to_end = jnp.exp(cum_t[length - 1 :, :] - cum_t)
    for tile in range(width // LANES):
        here = slice(LANES * tile, LANES * (tile + 1))
        dx_ref[:, here] = part_ref[:, here] + carried[:, here] * pair(to_end, tile, length)


def shifted(value, axis, step):
    count = lax.axis_size(axis)
    return lax.ppermute(value, axis, [(i, (i + step) % count) for i in range(count)])


def swapped(value, axis):
    return lax.ppermute(value, axis, [(i, i ^ 1) for i in range(lax.axis_size(axis))])


def exchange(value, axis):
    return lax.all_to_all(value, axis, 0, 0, tiled=True)


def per_device(head_input, gate_input, log_decay, in_b, in_c, skip, norm_gain, w_out, d_out):
    x, gate, ld, b_mat, c_mat, d_own = head_input[0], gate_input[0], log_decay.transpose(1, 0, 2), in_b[0], in_c[0], d_out[0]
    length, width = x.shape
    heads, state = ld.shape[0], b_mat.shape[1]
    model = w_out.shape[1]
    ranks, ring, seqs = lax.axis_size("ctx"), lax.axis_size("tp"), lax.axis_size("dp")
    block = d_own.shape[0]
    used = state * width // ranks // LANES
    pitch = -(-(used + 1) // 8) * 8
    pieces = (ranks * pitch, LANES)
    gain = norm_gain[None, :]
    dp = lax.axis_index("dp")
    pos = jnp.stack([lax.axis_index("tp"), lax.rem(lax.axis_index("ctx"), 2), dp]).astype(jnp.int32)
    half = model // 2
    chips = ranks // 2
    rows = model // ranks
    wide = max(width, 2 * rows)
    padded = -(-length // LANES) * LANES
    across = 4 if chips % 16 == 0 else 2
    down = chips // across
    lines = [[y * across + x for x in range(across)] for y in range(down)]
    lines = [
        [[2 * chip + c for chip in line] for line in way for c in range(2)] for way in (lines, list(zip(*lines)))
    ]

    d_prev, d_next = shifted(d_own, "tp", 1), shifted(d_own, "tp", -1)
    far_left, far_right = shifted(d_prev[:, :half], "tp", 1), shifted(d_next[:, half:], "tp", -1)

    send, cum, cum_t = call(
        functools.partial(block_state, ranks, pitch),
        [pieces, (heads, length), (length, heads)],
        [ld, x, b_mat],
        fixed=(0, 1, 2), name="block_state", us=0.3,
    )
    recv = exchange(send, "ctx")
    (y_local,) = call(
        functools.partial(local_output, heads),
        [(length, width)],
        [x, b_mat, c_mat, cum, cum_t, skip],
        smem=(5,), fixed=(0, 1, 2), name="local_output", us=0.3,
    )
    send, decays = call(
        functools.partial(scan_forward, ranks, pitch, used, width),
        [pieces, pieces],
        [recv],
        after=[y_local], far=(0, 1), name="scan_forward", us=0.3,
    )
    recv = exchange(send, "ctx")
    gated, normed, scale, part_left, part_right, part_next, part_prev, part_own = call(
        functools.partial(gate_out, ring, ranks, pitch),
        [(length, width)] * 2 + [(length, LANES)] + [(block, half)] * 2 + [(block, model)] * 3,
        [pos, recv, c_mat, cum_t, y_local, gate, gain, w_out],
        smem=(0,), tiled=7, fixed=(2, 5, 7), io=True, far=(3, 4, 5, 6, 7),
        scratch=[pltpu.VMEM((state, width), F32)] + [pltpu.VMEM((length, width), BF16)] * 2,
        name="gate_out", us=7,
    )
    up_far, down_far = shifted(part_left, "tp", 1), shifted(part_right, "tp", -1)
    keep, give, d_high, d_low = call(
        functools.partial(turn, ring, rows),
        [(half, padded), (half + width, padded)] + [jax.ShapeDtypeStruct((model, padded), BF16)] * 2,
        [pos, d_own, d_prev, d_next, far_left, far_right, normed],
        scratch=[pltpu.VMEM((padded, wide), F32), pltpu.VMEM((wide, padded), F32)],
        smem=(0,), name="turn", us=0.3,
    )
    other = swapped(give, "ctx")
    (d_normed,) = call(
        normed_grad, [(length, width)], [d_high, d_low, w_out],
        tiled=2, fixed=(2,), io=True, scratch=[pltpu.VMEM((width, padded), F32)], name="normed_grad", us=0.3,
    )
    (grad_w,) = call(
        functools.partial(weight_grad, across, down), [(half, width)], [keep, other, normed],
        scratch=[pltpu.VMEM((padded, width), BF16)] * 4,
        io=True, after=[d_normed], name="weight_grad", us=0.3,
    )
    whole = grad_w
    grad_w = lax.psum_scatter(grad_w, "ctx", scatter_dimension=0, tiled=True, axis_index_groups=lines[0])
    send, dy = call(
        functools.partial(norm_grad, ranks, pitch),
        [pieces, (length, width)],
        [d_normed, gated, scale, gate, gain, c_mat, cum_t],
        fixed=(3,), after=[whole], name="norm_grad", us=0.3,
    )
    recv = exchange(send, "ctx")
    (dx_local,) = call(
        functools.partial(local_grad, heads),
        [(length, width)],
        [dy, b_mat, c_mat, cum, cum_t, skip],
        smem=(5,), fixed=(1, 2), name="local_grad", us=0.3,
    )
    part_next, part_prev = call(
        pass_on, [(block, model)] * 2, [part_next, part_prev, up_far, down_far], fixed=(0, 1),
        after=[dx_local], name="pass_on", us=0.3,
    )
    up, low = shifted(part_next, "tp", 1), shifted(part_prev, "tp", -1)
    (send,) = call(
        functools.partial(scan_backward, ranks, pitch),
        [pieces],
        [recv, decays],
        fixed=(1,),
        after=[part_next], name="scan_backward", us=0.3,
    )
    recv = exchange(send, "ctx")
    (dx,) = call(
        functools.partial(finish, ranks, pitch),
        [(length, width)],
        [recv, b_mat, cum_t, dx_local],
        fixed=(1,),
        scratch=[pltpu.VMEM((state, width), F32)], name="finish", us=0.3,
    )
    out = part_own + up + low
    grad_w, *_ = lax.optimization_barrier((grad_w, dx, up, low))
    columns = [[seqs * i + p for i in line for p in range(seqs)] for line in lines[1]]
    grad_w = lax.all_to_all(grad_w, ("ctx", "dp"), 0, 0, tiled=True, axis_index_groups=columns)
    (share,) = call(
        functools.partial(sum_column, down * seqs), [(rows // seqs, width)], [grad_w],
        name="sum_column", us=1,
    )
    return (out[None], dx[None], share)


def solution(mesh):
    placed = (
        P("dp", "ctx", "tp"),
        P("dp", "ctx", "tp"),
        P("dp", "tp", "ctx"),
        P("dp", "ctx", None),
        P("dp", "ctx", None),
        P("tp"),
        P("tp"),
        P("tp", None),
        P("dp", ("ctx", "tp"), None),
    )
    return jax.shard_map(
        per_device,
        mesh=mesh,
        in_specs=placed,
        out_specs=(P("dp", ("ctx", "tp"), None), P("dp", "ctx", "tp"), P(("ctx", "dp"), "tp")),
        check_vma=False,
    )
```
